512 devices in a mesh: section: 8 (over y, z_hi), dp: 64 (over x, z_lo, core).
Axes of the slice: x: 4, y: 4, z: 16 (z_hi: 2, z_lo: 8; z = z_hi * 8 + z_lo), core: 2. Of those that a mesh axis runs over, the one named last changes fastest.
Arguments:
- first_acts: bfloat16 [4, 8192, 512], P(None, 'dp'), may hold values from -28 to 28
- cotangent: bfloat16 [4, 8192, 512], P(None, 'dp'), may hold values from -28 to 28
- weights: bfloat16 [4096, 512], P(('section', 'dp')), may hold values from -0.25 to 0.25
Outputs:
- update: float32 [4096, 512], P(('section', 'dp'))
The draws below stay inside these ranges and needn't reach their ends.
All inputs are finite; a program needn't handle non-finite values.
Results may differ from the reference program's by a relative error of at most 0.012.
The reference program's roundings to bfloat16 on the way count: a program that leaves them out, or rounds other values in their place, can miss the bound.
Values may be sent and summed in bfloat16 or wider, within the bound.
A program may use at most 64 MiB of HBM per device.

```python
import jax
import jax.numpy as jnp
from jax import lax

BLK = 512
TOK = 128
MB = 4
LAYERS = 8
N_DP = 64


def mixed_field(key, first, second):
    key_a, key_b = jax.random.split(key, 2)
    shape = (MB, N_DP * TOK, BLK)
    base = jnp.clip(jax.random.normal(key_a, shape, jnp.float32), -4.0, 4.0)
    mixed = base + first * jnp.roll(base, 1, axis=-1) + second * jnp.roll(base, 3, axis=-1)
    scales = jnp.exp(jax.random.uniform(key_b, (BLK,), jnp.float32, -1.2, 1.2))
    return mixed * scales


def draw_first_acts(key, part):
    key = jax.random.fold_in(key, 11)
    return mixed_field(key, 0.8, 0.5).astype(jnp.bfloat16)


def draw_cotangent(key, part):
    key = jax.random.fold_in(key, 23)
    return mixed_field(key, 0.7, -0.6).astype(jnp.bfloat16)


def steps_of(stream_key, extent, cuts, low, largest):
    factor_of = 1.0
    for axis_at, parts in cuts:
        steps = jax.random.uniform(jax.random.fold_in(jax.random.fold_in(stream_key, 6), axis_at), (parts,), jnp.float32, low / len(cuts), largest / len(cuts))
        factor_of = factor_of * jnp.repeat(jnp.exp(steps), extent[axis_at] // parts).reshape((-1,) + (1,) * (len(extent) - 1 - axis_at))
    return factor_of


def noise(rng, shape, deviation, reach, shards=(), kind=jnp.bfloat16):
    drawn = deviation * jax.random.normal(rng, shape, jnp.float32)
    if shards:
        drawn = drawn * steps_of(rng, shape, shards, -0.22, 0.18)
    return jnp.clip(drawn, -reach, reach).astype(kind)


def setup_inputs(seed: int = 0) -> dict:
    streams_of = jax.random.split(jax.random.key(seed), 4)
    return {
        "first_acts": draw_first_acts(jax.random.fold_in(streams_of[3], 71), 0),
        "cotangent": draw_cotangent(jax.random.fold_in(streams_of[3], 71), 0),
        "weights": noise(streams_of[2], (LAYERS * BLK, BLK), BLK ** -0.5, 0.25, ((0, 512),)),
    }


def gelu_parts(h):
    coeff = 0.7978845608028654
    inner = coeff * (h + 0.044715 * h * h * h)
    tanh_val = jnp.tanh(inner)
    value = 0.5 * h * (1.0 + tanh_val)
    slope = 0.5 * (1.0 + tanh_val) + 0.5 * h * (1.0 - tanh_val * tanh_val) * coeff * (1.0 + 3.0 * 0.044715 * h * h)
    return (value, slope)

def normed(x_val):
    xf = x_val.astype(jnp.float32)
    scale = lax.rsqrt(lax.optimization_barrier(jnp.mean(xf * xf, axis=-1, keepdims=True)) + 1e-05)
    return (xf, scale, (xf * scale).astype(jnp.bfloat16))

def cholesky_apply(factor, rhs):
    half = lax.linalg.triangular_solve(factor, rhs, left_side=True, lower=True)
    return lax.linalg.triangular_solve(factor, half, left_side=True, lower=True, transpose_a=True)

def reference(first_acts, cotangent, weights):
    width = weights.shape[1]
    layers = weights.shape[0] // width
    count = first_acts.shape[0] * first_acts.shape[1]
    saved = []
    x_val = first_acts
    for layer in range(layers):
        w_mat = weights[layer * width:(layer + 1) * width]
        saved.append(x_val)
        xf, scale, unit = normed(x_val)
        h_val = jnp.dot(unit.astype(jnp.float32), w_mat.astype(jnp.float32), preferred_element_type=jnp.float32)
        value, slope = gelu_parts(h_val)
        x_val = (xf + value).astype(jnp.bfloat16)
    grad = cotangent
    results = [None] * layers
    eye = jnp.eye(width, dtype=jnp.float32)
    for layer in reversed(range(layers)):
        w_mat = weights[layer * width:(layer + 1) * width]
        xf, scale, unit = normed(saved[layer])
        h_val = jnp.dot(unit.astype(jnp.float32), w_mat.astype(jnp.float32), preferred_element_type=jnp.float32)
        value, slope = gelu_parts(h_val)
        d_h = (grad.astype(jnp.float32) * slope).astype(jnp.bfloat16)
        unit_flat = unit.reshape(-1, width)
        dh_flat = d_h.reshape(-1, width)
        gram_in = jnp.dot(unit_flat.T.astype(jnp.float32), unit_flat.astype(jnp.float32), preferred_element_type=jnp.float32) / count + 0.1 * eye
        gram_out = jnp.dot(dh_flat.T.astype(jnp.float32), dh_flat.astype(jnp.float32), preferred_element_type=jnp.float32) / count + 0.1 * eye
        grad_w = jnp.dot(unit_flat.T.astype(jnp.float32), dh_flat.astype(jnp.float32), preferred_element_type=jnp.float32)
        d_u = jnp.dot(d_h.astype(jnp.float32), w_mat.T.astype(jnp.float32), preferred_element_type=jnp.float32)
        back = scale * d_u - xf * scale * scale * scale * lax.optimization_barrier(jnp.mean(d_u * xf, axis=-1, keepdims=True))
        grad = (grad.astype(jnp.float32) + back).astype(jnp.bfloat16)
        chol_in = jnp.linalg.cholesky(gram_in)
        chol_out = jnp.linalg.cholesky(gram_out)
        left = cholesky_apply(chol_in, grad_w)
        precond = cholesky_apply(chol_out, left.T).T
        results[layer] = precond / jnp.sqrt(jnp.mean(precond * precond) + 1e-06)
    return jnp.concatenate(results, axis=0)
```

```python
import jax
import jax.numpy as jnp
from jax import lax
from jax.experimental import pallas as pl
from jax.experimental.pallas import tpu as pltpu
from jax.sharding import PartitionSpec as P

MESH = pl.DeviceIdType.MESH
HIGHEST = lax.Precision.HIGHEST
WIDTH = 512
TOKENS = 512
LAYERS = 8
CHUNKS = 128
ROWS = 40
VMEM_LIMIT = 56 * 1024 * 1024


def place():
    section = lax.axis_index("section")
    rank = lax.axis_index("dp")
    y, z_hi = section // 2, section % 2
    x, z_lo, core = rank // 16, (rank % 16) // 2, rank % 2
    return x, y, z_hi, z_lo, core


def device(x, y, z_hi, z_lo, core):
    return (y * 2 + z_hi, x * 16 + z_lo * 2 + core)


def flip_low(v):
    return v + 1 - 2 * (v % 2)


def send(src, dst, send_sem, recv_sem, target):
    copy = pltpu.make_async_remote_copy(
        src_ref=src, dst_ref=dst, send_sem=send_sem, recv_sem=recv_sem,
        device_id=target, device_id_type=MESH,
    )
    copy.start()
    return copy


def meet(targets):
    barrier = pltpu.get_barrier_semaphore()
    for target in targets:
        pl.semaphore_signal(barrier, inc=1, device_id=target, device_id_type=MESH)
    pl.semaphore_wait(barrier, len(targets))


def gather_kernel(w_ref, buf, mine_ref, sib_ref, sib_sem, z_send, z_recv, h_send, h_recv, c_send, c_recv):
    x, y, z_hi, z_lo, core = place()
    z = z_hi * 8 + z_lo
    sibling = device(x, y, z_hi, z_lo, 1 - core)
    z_peers = []
    for k in range(1, 16):
        other = (z + k) % 16
        z_peers.append(device(x, y, other // 8, other % 8, core))
    moves = [
        (lambda a, b: (flip_low(a), b)),
        (lambda a, b: (3 - a, b)),
        (lambda a, b: (a, flip_low(b))),
        (lambda a, b: (a, 3 - b)),
    ]
    orders = [(0, 1, 2, 3), (1, 2, 3, 0), (2, 3, 0, 1), (3, 0, 1, 2)]
    partners = []
    for move in moves:
        px, py = move(x, y)
        partners.append(device(px, py, z_hi, z_lo, core))
    meet([sibling] + z_peers + partners)

    first = core == 0
    wf = w_ref[...].astype(jnp.float32)
    left, right = wf[:, :256], wf[:, 256:]
    mine_ref[...] = jnp.where(first, right, left)
    swap = send(mine_ref, sib_ref, sib_sem.at[0], sib_sem.at[1], sibling)
    mine = jnp.where(first, left, right)
    swap.wait()
    theirs = sib_ref[...]
    rows = jnp.concatenate([jnp.where(first, mine, theirs), jnp.where(first, theirs, mine)], axis=0)
    own = buf.at[core, y, z_hi, x, pl.ds(pl.multiple_of(z_lo * 16, 16), 16), :]
    own[...] = rows.astype(jnp.bfloat16)
    z_copies = [send(own, own, z_send.at[k], z_recv.at[k], z_peers[k - 1]) for k in range(1, 16)]
    for copy in z_copies:
        copy.wait_recv()

    def block(j, at):
        bx, by = at
        return buf.at[core, by, j // 2, bx, pl.ds((j % 2) * 64, 64), :]

    held = {}
    copies = {}
    across = {}

    def forward(j, r, step_from):
        ref = block(j, held[j, r])
        for step in range(step_from, 4):
            index = 2 ** step + r
            copies[j, index] = send(
                ref, ref, h_send.at[j, index], h_recv.at[j, index], partners[orders[j][step]]
            )
        across[j, r] = send(ref, ref, c_send.at[j, r], c_recv.at[j, r], sibling)

    for j in range(4):
        held[j, 0] = (x, y)
        for r in range(1, 16):
            step = r.bit_length() - 1
            held[j, r] = moves[orders[j][step]](*held[j, r - 2 ** step])
    for j in range(4):
        forward(j, 0, 0)
    arrivals = sorted(range(1, 16), key=lambda r: (bin(r).count("1"), r))
    for r in arrivals:
        for j in range(4):
            copies[j, r].wait_recv()
            forward(j, r, r.bit_length())
    for j in range(4):
        for r in range(16):
            across[j, r].wait_recv()
    for copy in z_copies:
        copy.wait_send()
    for j in range(4):
        for r in range(16):
            across[j, r].wait_send()
            if r:
                copies[j, r].wait_send()


def gather(weights):
    return pl.pallas_call(
        gather_kernel,
        out_shape=jax.ShapeDtypeStruct((2, 4, 2, 4, 128, 256), jnp.bfloat16),
        in_specs=[pl.BlockSpec(memory_space=pltpu.VMEM)],
        out_specs=pl.BlockSpec(memory_space=pltpu.VMEM),
        scratch_shapes=[
            pltpu.VMEM((8, 256), jnp.float32),
            pltpu.VMEM((8, 256), jnp.float32),
            pltpu.SemaphoreType.DMA((2,)),
            pltpu.SemaphoreType.DMA((16,)),
            pltpu.SemaphoreType.DMA((16,)),
            pltpu.SemaphoreType.DMA((4, 16)),
            pltpu.SemaphoreType.DMA((4, 16)),
            pltpu.SemaphoreType.DMA((4, 16)),
            pltpu.SemaphoreType.DMA((4, 16)),
        ],
        compiler_params=pltpu.CompilerParams(
            collective_id=0, has_side_effects=True, vmem_limit_bytes=VMEM_LIMIT
        ),
        name="weights_gather",
    )(weights)


def gelu_parts(h):
    coeff = 0.7978845608028654
    inner = coeff * (h + 0.044715 * h * h * h)
    tanh_val = jnp.tanh(inner)
    value = 0.5 * h * (1.0 + tanh_val)
    slope = 0.5 * (1.0 + tanh_val) + 0.5 * h * (1.0 - tanh_val * tanh_val) * coeff * (
        1.0 + 3.0 * 0.044715 * h * h
    )
    return (value, slope)


def dot(a, b, dims, precision=None):
    return lax.dot_general(
        a, b, ((dims[:1], dims[1:]), ((), ())), precision=precision,
        preferred_element_type=jnp.float32,
    )


SPLIT = 128


def chain_kernel(act_ref, cot_ref, w_ref, out_ref, xs, slopes, scales, grads, u_own, dh_own):
    section = lax.axis_index("section")
    parts = TOKENS // SPLIT
    xs[0] = act_ref[...]
    grads[...] = cot_ref[...]

    def ahead(layer, carry):
        for part in range(parts):
            rows = pl.ds(part * SPLIT, SPLIT)
            xf = xs[layer, rows, :].astype(jnp.float32)
            scale = lax.rsqrt(jnp.mean(xf * xf, axis=-1, keepdims=True) + 1e-05)
            scales[layer, rows, :] = jnp.broadcast_to(scale, (SPLIT, 128))
            unit = (xf * scale).astype(jnp.bfloat16)

            @pl.when(layer == section)
            def _():
                u_own[rows, :] = unit

            for half in range(2):
                columns = pl.ds(half * 256, 256)
                h_val = dot(unit, w_ref[half, layer], (1, 0))
                value, slope = gelu_parts(h_val)
                slopes[layer, rows, columns] = slope
                xs[layer + 1, rows, columns] = (xf[:, half * 256:half * 256 + 256] + value).astype(jnp.bfloat16)
        return carry

    lax.fori_loop(0, LAYERS, ahead, 0)

    def back(step, carry):
        layer = LAYERS - 1 - step
        for part in range(parts):
            rows = pl.ds(part * SPLIT, SPLIT)
            grad = grads[rows, :].astype(jnp.float32)
            d_h = (grad * slopes[layer, rows, :]).astype(jnp.bfloat16)

            @pl.when(layer == section)
            def _():
                dh_own[rows, :] = d_h

            d_u = dot(d_h[:, :256], w_ref[0, layer], (1, 1)) + dot(d_h[:, 256:], w_ref[1, layer], (1, 1))
            xf = xs[layer, rows, :].astype(jnp.float32)
            scale = scales[layer, rows, 0:1]
            shift = scale * scale * scale * jnp.mean(d_u * xf, axis=-1, keepdims=True)
            grads[rows, :] = (grad + (scale * d_u - xf * shift)).astype(jnp.bfloat16)
        return carry

    lax.fori_loop(0, LAYERS, back, 0)

    def keep(at, value):
        for half in range(value.shape[1] // 128):
            out_ref[at + half] = value[:, half * 128:half * 128 + 128]

    for base, ref in ((0, u_own), (6, dh_own)):
        for at, low, high in ((0, 0, 0), (2, 256, 0), (4, 256, 256)):
            keep(base + at, dot(ref[:, low:low + 256], ref[:, high:high + 256], (0, 0)))
    for top in range(2):
        keep(12 + 4 * top, dot(u_own[:, top * 256:top * 256 + 256], dh_own[...], (0, 0)))


def chain(acts, cots, w_all):
    return pl.pallas_call(
        chain_kernel,
        out_shape=jax.ShapeDtypeStruct((20, 256, 128), jnp.float32),
        in_specs=[pl.BlockSpec(memory_space=pltpu.VMEM)] * 3,
        out_specs=pl.BlockSpec(memory_space=pltpu.VMEM),
        scratch_shapes=[
            pltpu.VMEM((LAYERS + 1, TOKENS, WIDTH), jnp.bfloat16),
            pltpu.VMEM((LAYERS, TOKENS, WIDTH), jnp.float32),
            pltpu.VMEM((LAYERS, TOKENS, 128), jnp.float32),
            pltpu.VMEM((TOKENS, WIDTH), jnp.bfloat16),
            pltpu.VMEM((TOKENS, WIDTH), jnp.bfloat16),
            pltpu.VMEM((TOKENS, WIDTH), jnp.bfloat16),
        ],
        compiler_params=pltpu.CompilerParams(vmem_limit_bytes=VMEM_LIMIT),
        name="layer_chain",
    )(acts, cots, w_all)


def reduce_kernel(part_ref, out_ref, acc, got_core, got_x1, got_x2, got_z1, got_z2, got_z4, sems):
    x, y, z_hi, z_lo, core = place()
    x_low, x_high = ((x + 1) // 2) % 2, x // 2
    z_bits = (z_lo % 2, (z_lo // 2) % 2, z_lo // 4)
    sibling = device(x, y, z_hi, z_lo, 1 - core)
    x_low_peer = device(flip_low(x), y, z_hi, z_lo, core)
    x_high_peer = device(3 - x, y, z_hi, z_lo, core)
    z_peers = []
    for bit, distance in zip(z_bits, (1, 2, 4)):
        z_peers.append(device(x, y, z_hi, z_lo + distance * (1 - 2 * bit), core))
    meet([sibling, x_low_peer, x_high_peer] + z_peers)

    copies = []

    def move(step, sub, src, dst, target):
        copy = send(src, dst, sems.at[0, step, sub], sems.at[1, step, sub], target)
        copies.append(copy)
        return copy

    swap = move(0, 0, part_ref.at[pl.ds((1 - core) * 64, 64)], got_core, sibling)
    swap.wait_recv()
    acc[...] = part_ref[pl.ds(core * 64, 64)] + got_core[...]

    order = [
        [(x_low, x_low_peer), (x_high, x_high_peer)],
        [(x_high, x_high_peer), (x_low, x_low_peer)],
    ]
    for sub in range(2):
        order[sub] += list(zip(z_bits, z_peers))
    base = [0, 32]
    for step in range(5):
        size = 16 >> step
        got = (got_x1, got_x2, got_z1, got_z2, got_z4)[step]
        waits = []
        for sub in range(2):
            bit, peer = order[sub][step]
            waits.append(move(1 + step, sub, acc.at[pl.ds(base[sub] + (1 - bit) * size, size)], got.at[sub], peer))
            base[sub] = base[sub] + bit * size
        for sub in range(2):
            waits[sub].wait_recv()
            mine = pl.ds(base[sub], size)
            acc[mine] = acc[mine] + got[sub]
    final = [core * 64 + base[sub] for sub in range(2)]
    for sub in range(2):
        out_ref[pl.ds(final[sub], 1)] = acc[pl.ds(base[sub], 1)]
    for step in reversed(range(5)):
        size = 16 >> step
        waits = []
        for sub in range(2):
            bit, peer = order[sub][step]
            mine = out_ref.at[pl.ds(final[sub], size)]
            waits.append(move(6 + step, sub, mine, mine, peer))
            final[sub] = final[sub] - bit * size
        for sub in range(2):
            waits[sub].wait_recv()
    waits = []
    for sub in range(2):
        mine = out_ref.at[pl.ds(core * 64 + sub * 32, 32)]
        waits.append(move(11, sub, mine, mine, sibling))
    for sub in range(2):
        waits[sub].wait_recv()
    for copy in copies:
        copy.wait_send()


def reduce_all(partial):
    chunk = lambda *lead: pltpu.VMEM(lead + (ROWS, 128), jnp.float32)
    return pl.pallas_call(
        reduce_kernel,
        out_shape=jax.ShapeDtypeStruct((CHUNKS, ROWS, 128), jnp.float32),
        in_specs=[pl.BlockSpec(memory_space=pltpu.VMEM)],
        out_specs=pl.BlockSpec(memory_space=pltpu.VMEM),
        scratch_shapes=[
            chunk(64), chunk(64), chunk(2, 16), chunk(2, 8), chunk(2, 4), chunk(2, 2), chunk(2, 1),
            pltpu.SemaphoreType.DMA((2, 12, 2)),
        ],
        compiler_params=pltpu.CompilerParams(
            collective_id=1, has_side_effects=True, vmem_limit_bytes=VMEM_LIMIT
        ),
        name="sums_reduce",
    )(partial)


def splat(value):
    return jnp.broadcast_to(value, (8, 128))


def panel_step(tiles):
    pivot = tiles[0]
    lane = lax.broadcasted_iota(jnp.int32, (8, 128), 1)
    row = lax.broadcasted_iota(jnp.int32, (8, 128), 0)
    columns = [splat(pivot[:, k:k + 1]) for k in range(8)]
    e = {}
    for k in range(8):
        for i in range(k + 1):
            e[i, k] = splat(columns[k][i:i + 1, :])
    at = lambda i, k: (min(i, k), max(i, k))
    for k in range(8):
        inverse = 1.0 / e[k, k]
        scaled = {i: e[at(i, k)] * inverse for i in range(8) if i != k}
        for i in range(8):
            for j in range(i, 8):
                if i != k and j != k:
                    e[i, j] = e[i, j] - e[at(i, k)] * scaled[j]
        for i in scaled:
            e[at(i, k)] = scaled[i]
        e[k, k] = -inverse
    in_block = lane < 8
    top = jnp.where(in_block, jnp.where(lane == row, 1.0, 0.0), pivot)
    result = None
    for k in range(8):
        column = e[at(0, k)]
        for i in range(1, 8):
            column = jnp.where(row == i, e[at(i, k)], column)
        term = column * splat(top[k:k + 1, :])
        result = -term if result is None else result - term
    spread = [splat(result[k:k + 1, :]) for k in range(8)]
    moved = []
    for tile in tiles[1:]:
        value = jnp.where(in_block, 0.0, tile)
        for k in range(8):
            value = value - splat(tile[:, k:k + 1]) * spread[k]
        moved.append(value)
    moved.append(result)
    return [pltpu.roll(tile, 120, 1) for tile in moved]


def solve_kernel(sum_ref, out_ref, mats, d_mat, p_mat):
    rank = lax.axis_index("dp")
    row = lax.broadcasted_iota(jnp.int32, (WIDTH, WIDTH), 0)
    lane = lax.broadcasted_iota(jnp.int32, (WIDTH, WIDTH), 1)
    shift = jnp.where(row == lane, 0.1, 0.0)
    for which in range(2):
        base = 6 * which
        for half in range(2):
            columns = slice(half * 128, half * 128 + 128)
            mats[which, :256, columns] = sum_ref[base + half]
            mats[which, 256:, columns] = sum_ref[base + 2 + half]
            mats[which, columns, 256:] = sum_ref[base + 2 + half].T
            mats[which, 256:, 256 + half * 128:384 + half * 128] = sum_ref[base + 4 + half]
        mats[which] = mats[which] * (1.0 / 32768.0) + shift
    for top in range(2):
        for quarter in range(4):
            d_mat[top * 256:top * 256 + 256, quarter * 128:quarter * 128 + 128] = sum_ref[12 + 4 * top + quarter]

    block_row = lax.broadcasted_iota(jnp.int32, (128, 128), 0)
    block_lane = lax.broadcasted_iota(jnp.int32, (128, 128), 1)
    unit = jnp.where(block_row == block_lane, 1.0, 0.0)
    for k in range(4):
        span = slice(k * 128, k * 128 + 128)
        start = []
        for which in range(2):
            for i in range(16):
                start.append(mats[which, k * 128 + i * 8:k * 128 + i * 8 + 8, span])

        def advance(step, tiles):
            return tuple(panel_step(list(tiles[:16])) + panel_step(list(tiles[16:])))

        done = lax.fori_loop(0, 16, advance, tuple(start))
        for which in range(2):
            inverse = jnp.concatenate(done[16 * which:16 * which + 16], axis=0)
            side = mats[which, :, span]
            mats[which, :, span] = jnp.zeros((WIDTH, 128), jnp.float32)
            mats[which, span, span] = unit
            top = dot(inverse, mats[which, span, :], (1, 0), HIGHEST)
            for i in range(4):
                here = slice(i * 128, i * 128 + 128)
                if i == k:
                    mats[which, here, :] = top
                else:
                    mats[which, here, :] = mats[which, here, :] - dot(side[here], top, (1, 0), HIGHEST)
    p_mat[...] = dot(mats[0], d_mat[...], (1, 0), HIGHEST)
    p_mat[...] = dot(p_mat[...], mats[1], (1, 0), HIGHEST)
    whole = p_mat[...]
    mean = jnp.sum(jnp.sum(whole * whole, axis=0, keepdims=True), axis=1, keepdims=True) * (1.0 / (WIDTH * WIDTH))
    mine = p_mat[pl.ds(pl.multiple_of(rank * 8, 8), 8), :]
    out_ref[...] = mine / jnp.sqrt(mean + 1e-06)


def solve(sums):
    square = pltpu.VMEM((WIDTH, WIDTH), jnp.float32)
    return pl.pallas_call(
        solve_kernel,
        out_shape=jax.ShapeDtypeStruct((8, WIDTH), jnp.float32),
        in_specs=[pl.BlockSpec(memory_space=pltpu.VMEM)],
        out_specs=pl.BlockSpec(memory_space=pltpu.VMEM),
        scratch_shapes=[pltpu.VMEM((2, WIDTH, WIDTH), jnp.float32), square, square],
        compiler_params=pltpu.CompilerParams(vmem_limit_bytes=VMEM_LIMIT),
        name="factor_solve",
    )(sums)


def local(first_acts, cotangent, weights):
    w_all = gather(weights).reshape(2, LAYERS, WIDTH, 256)
    partial = chain(first_acts.reshape(TOKENS, WIDTH), cotangent.reshape(TOKENS, WIDTH), w_all)
    sums = reduce_all(partial.reshape(CHUNKS, ROWS, 128)).reshape(20, 256, 128)
    return solve(sums)


def solution(mesh):
    placed = (P(None, "dp", None), P(None, "dp", None), P(("section", "dp"), None))
    return jax.shard_map(
        local, mesh=mesh, in_specs=placed, out_specs=P(("section", "dp"), None), check_vma=False
    )
```

```python
import functools

import jax
import jax.numpy as jnp
from jax import lax
from jax.experimental import pallas as pl
from jax.experimental.pallas import tpu as pltpu
from jax.sharding import PartitionSpec as P

MESH = pl.DeviceIdType.MESH
WIDTH = 512
TOKENS = 512
LAYERS = 8
HALF = 256
VMEM_LIMIT = 56 * 1024 * 1024


def place():
    section = lax.axis_index("section")
    rank = lax.axis_index("dp")
    y, z_hi = section // 2, section % 2
    x, z_lo, core = rank // 16, (rank % 16) // 2, rank % 2
    return x, y, z_hi, z_lo, core


def device(x, y, z_hi, z_lo, core):
    return (y * 2 + z_hi, x * 16 + z_lo * 2 + core)


def flip_low(v):
    return v + 1 - 2 * (v % 2)


def send(src, dst, send_sem, recv_sem, target):
    copy = pltpu.make_async_remote_copy(
        src_ref=src, dst_ref=dst, send_sem=send_sem, recv_sem=recv_sem,
        device_id=target, device_id_type=MESH,
    )
    copy.start()
    return copy


def meet(targets):
    barrier = pltpu.get_barrier_semaphore()
    for target in targets:
        pl.semaphore_signal(barrier, inc=1, device_id=target, device_id_type=MESH)
    pl.semaphore_wait(barrier, len(targets))


def gather_weights(w_ref, buf, mine_ref, sib_ref, sib_sem, z_send, z_recv, h_send, h_recv, c_send, c_recv):
    x, y, z_hi, z_lo, core = place()
    z = z_hi * 8 + z_lo
    sibling = device(x, y, z_hi, z_lo, 1 - core)
    z_peers = []
    for k in range(1, 16):
        other = (z + k) % 16
        z_peers.append(device(x, y, other // 8, other % 8, core))
    moves = [
        (lambda a, b: (flip_low(a), b)),
        (lambda a, b: (3 - a, b)),
        (lambda a, b: (a, flip_low(b))),
        (lambda a, b: (a, 3 - b)),
    ]
    orders = [(0, 1, 2, 3), (1, 2, 3, 0), (2, 3, 0, 1), (3, 0, 1, 2)]
    partners = []
    for move in moves:
        px, py = move(x, y)
        partners.append(device(px, py, z_hi, z_lo, core))
    meet([sibling] + z_peers + partners)

    first = core == 0
    wf = w_ref[...].astype(jnp.float32)
    left, right = wf[:, :256], wf[:, 256:]
    mine_ref[...] = jnp.where(first, right, left)
    swap = send(mine_ref, sib_ref, sib_sem.at[0], sib_sem.at[1], sibling)
    mine = jnp.where(first, left, right)
    swap.wait()
    theirs = sib_ref[...]
    rows = jnp.concatenate([jnp.where(first, mine, theirs), jnp.where(first, theirs, mine)], axis=0)
    own = buf.at[core, y, z_hi, x, pl.ds(pl.multiple_of(z_lo * 16, 16), 16), :]
    own[...] = rows.astype(jnp.bfloat16)
    z_copies = [send(own, own, z_send.at[k], z_recv.at[k], z_peers[k - 1]) for k in range(1, 16)]
    for copy in z_copies:
        copy.wait_recv()

    def block(j, at):
        bx, by = at
        return buf.at[core, by, j // 2, bx, pl.ds((j % 2) * 64, 64), :]

    held = {}
    copies = {}
    across = {}

    def forward(j, r, step_from):
        ref = block(j, held[j, r])
        for step in range(step_from, 4):
            index = 2 ** step + r
            copies[j, index] = send(
                ref, ref, h_send.at[j, index], h_recv.at[j, index], partners[orders[j][step]]
            )
        across[j, r] = send(ref, ref, c_send.at[j, r], c_recv.at[j, r], sibling)

    for j in range(4):
        held[j, 0] = (x, y)
        for r in range(1, 16):
            step = r.bit_length() - 1
            held[j, r] = moves[orders[j][step]](*held[j, r - 2 ** step])
    for j in range(4):
        forward(j, 0, 0)
    arrivals = sorted(range(1, 16), key=lambda r: (bin(r).count("1"), r))
    for r in arrivals:
        for j in range(4):
            copies[j, r].wait_recv()
            forward(j, r, r.bit_length())
    for j in range(4):
        for r in range(16):
            across[j, r].wait_recv()
    for copy in z_copies:
        copy.wait_send()
    for j in range(4):
        for r in range(16):
            across[j, r].wait_send()
            if r:
                copies[j, r].wait_send()


def gelu_parts(h):
    coeff = 0.7978845608028654
    inner = coeff * (h + 0.044715 * h * h * h)
    tanh_val = jnp.tanh(inner)
    value = 0.5 * h * (1.0 + tanh_val)
    slope = 0.5 * (1.0 + tanh_val) + 0.5 * h * (1.0 - tanh_val * tanh_val) * coeff * (
        1.0 + 3.0 * 0.044715 * h * h
    )
    return (value, slope)


def dot(a, b, dims):
    return lax.dot_general(
        a, b, ((dims[:1], dims[1:]), ((), ())), preferred_element_type=jnp.float32
    )


def splat(value):
    return jnp.broadcast_to(value, (8, 128))


def thirds(value):
    high = value.astype(jnp.bfloat16).astype(jnp.float32)
    rest = value - high
    middle = rest.astype(jnp.bfloat16).astype(jnp.float32)
    return high, middle, rest - middle


def product(a, b, dims, axes):
    a0, a1, a2 = thirds(a)
    b0, b1, b2 = thirds(b)
    long_a = jnp.concatenate([a0, a0, a1, a1, a0, a2], axis=axes[0]).astype(jnp.bfloat16)
    long_b = jnp.concatenate([b0, b1, b0, b1, b2, b0], axis=axes[1]).astype(jnp.bfloat16)
    return dot(long_a, long_b, dims)


def minus_inverse(e):
    at = lambda i, k: (min(i, k), max(i, k))
    for k in range(0, 8, 2):
        a, b, c = e[k, k], e[k, k + 1], e[k + 1, k + 1]
        scale = 1.0 / (a * c - b * b)
        ia, ib, ic = c * scale, -(b * scale), a * scale
        others = [i for i in range(8) if i not in (k, k + 1)]
        r0 = {i: ia * e[at(i, k)] + ib * e[at(i, k + 1)] for i in others}
        r1 = {i: ib * e[at(i, k)] + ic * e[at(i, k + 1)] for i in others}
        for i in others:
            for j in others:
                if i <= j:
                    e[i, j] = e[i, j] - (e[at(i, k)] * r0[j] + e[at(i, k + 1)] * r1[j])
        for i in others:
            e[at(i, k)], e[at(i, k + 1)] = r0[i], r1[i]
        e[k, k], e[k, k + 1], e[k + 1, k + 1] = -ia, -ib, -ic
    return lambda i, k: e[at(i, k)]


def sweep_pair(tiles):
    tiles = list(tiles)
    lane = lax.broadcasted_iota(jnp.int32, (8, 128), 1)
    row = lax.broadcasted_iota(jnp.int32, (8, 128), 0)
    first = lane < 64
    local_lane = lane % 64

    def column(tile, k):
        return jnp.where(first, splat(tile[:, k:k + 1]), splat(tile[:, 64 + k:65 + k]))

    for p in range(8):
        pivot = tiles[p]
        base = 8 * p
        in_block = (local_lane >= base) & (local_lane < base + 8)
        columns = [column(pivot, base + k) for k in range(8)]
        e = {}
        for k in range(8):
            for i in range(k + 1):
                e[i, k] = splat(columns[k][i:i + 1, :])
        inverse = minus_inverse(e)
        top = jnp.where(in_block, jnp.where(local_lane - base == row, 1.0, 0.0), -pivot)
        result = None
        for k in range(8):
            spread = inverse(0, k)
            for i in range(1, 8):
                spread = jnp.where(row == i, inverse(i, k), spread)
            term = spread * splat(top[k:k + 1, :])
            result = term if result is None else result + term
        tiles[p] = result
        if p < 7:
            value = jnp.where(in_block, 0.0, tiles[p + 1])
            for k in range(8):
                value = value - column(tiles[p + 1], base + k) * splat(result[k:k + 1, :])
        update = product(pivot, result, (0, 0), (0, 0))
        for i in range(8):
            if i not in (p, p + 1):
                step = jnp.where(first, update[8 * i:8 * i + 8], update[64 + 8 * i:72 + 8 * i])
                tiles[i] = jnp.where(in_block, 0.0, tiles[i]) - step
        if p < 7:
            tiles[p + 1] = value
    return tiles


def run_ahead(w_buf, xs, slopes, scales, u_own):
    section = lax.axis_index("section")

    def ahead(layer, carry):
        xf = xs[layer].astype(jnp.float32)
        scale = lax.rsqrt(jnp.mean(xf * xf, axis=-1, keepdims=True) + 1e-05)
        scales[layer] = jnp.broadcast_to(scale, (TOKENS, 128))
        unit = (xf * scale).astype(jnp.bfloat16)

        @pl.when(layer == section)
        def _():
            u_own[...] = unit

        for half in range(2):
            columns = slice(half * HALF, half * HALF + HALF)
            w_half = w_buf[half, layer // 2, layer % 2].reshape(WIDTH, HALF)
            value, slope = gelu_parts(dot(unit, w_half, (1, 0)))
            slopes[layer, :, columns] = slope
            xs[layer + 1, :, columns] = (xf[:, columns] + value).astype(jnp.bfloat16)
        return carry

    lax.fori_loop(0, LAYERS, ahead, 0)


def run_back(w_buf, xs, slopes, scales, grads, dh_own, beside):
    section = lax.axis_index("section")

    def back(step, carry):
        beside(step)
        layer = LAYERS - 1 - step
        grad = grads[...].astype(jnp.float32)
        d_h = (grad * slopes[layer]).astype(jnp.bfloat16)

        @pl.when(layer == section)
        def _():
            dh_own[...] = d_h

        d_u = None
        for half in range(2):
            w_half = w_buf[half, layer // 2, layer % 2].reshape(WIDTH, HALF)
            term = dot(d_h[:, half * HALF:half * HALF + HALF], w_half, (1, 1))
            d_u = term if d_u is None else d_u + term
        xf = xs[layer].astype(jnp.float32)
        scale = scales[layer, :, 0:1]
        shift = scale * scale * scale * jnp.mean(d_u * xf, axis=-1, keepdims=True)
        grads[...] = (grad + (scale * d_u - xf * shift)).astype(jnp.bfloat16)
        return carry

    lax.fori_loop(0, LAYERS, back, 0)


def keep(ref, at, value):
    for i in range(value.shape[1] // 128):
        ref[at + i * HALF:at + i * HALF + HALF, :] = value[:, i * 128:i * 128 + 128]


class Stream:
    def __init__(self, index, refs, sems, swap_x):
        self.part, self.acc, self.full, *self.got = refs
        self.sems, self.index = sems, index
        self.rows = self.part.shape[0]
        x, y, z_hi, z_lo, core = place()
        self.core = core
        self.sibling = device(x, y, z_hi, z_lo, 1 - core)
        steps = [
            (((x + 1) // 2) % 2, device(flip_low(x), y, z_hi, z_lo, core)),
            (x // 2, device(3 - x, y, z_hi, z_lo, core)),
        ]
        if swap_x:
            steps.reverse()
        for bit, distance in ((z_lo % 2, 1), ((z_lo // 2) % 2, 2), (z_lo // 4, 4)):
            steps.append((bit, device(x, y, z_hi, z_lo + distance * (1 - 2 * bit), core)))
        base = 0
        self.sent, self.kept, self.peers = [0], [0], [self.sibling]
        for t, (bit, peer) in enumerate(steps, 1):
            size = self.rows // 2 >> t
            self.sent.append(base + (1 - bit) * size)
            base = base + bit * size
            self.kept.append(base)
            self.peers.append(peer)

    def span(self, at, size):
        return pl.ds(pl.multiple_of(at, 8), size)

    def copy(self, t):
        half = self.rows // 2
        if t == 0:
            src, dst, peer = self.part.at[self.span((1 - self.core) * half, half)], self.got[0], self.sibling
        elif t <= 5:
            size = half >> t
            src, dst, peer = self.acc.at[self.span(self.sent[t], size)], self.got[t], self.peers[t]
        else:
            k = 11 - t
            src = self.full.at[self.span(self.core * half + self.kept[k], half >> k)]
            dst, peer = src, self.peers[k]
        return pltpu.make_async_remote_copy(
            src_ref=src, dst_ref=dst, send_sem=self.sems.at[0, self.index, t],
            recv_sem=self.sems.at[1, self.index, t], device_id=peer, device_id_type=MESH,
        )

    def advance(self, t):
        half = self.rows // 2
        if t > 0:
            done = t - 1
            self.copy(done).wait_recv()
            if done == 0:
                self.acc[...] = self.part[self.span(self.core * half, half), :] + self.got[0][...]
            elif done <= 5:
                mine = self.span(self.kept[done], half >> done)
                total = self.acc[mine, :] + self.got[done][...]
                if done < 5:
                    self.acc[mine, :] = total
                else:
                    self.full[self.span(self.core * half + self.kept[5], half >> 5), :] = total
        if t < 12:
            self.copy(t).start()

    def close(self):
        for t in range(12):
            self.copy(t).wait_send()


def load_factor(mats, which, small, large):
    row = lax.broadcasted_iota(jnp.int32, (128, 128), 0)
    lane = lax.broadcasted_iota(jnp.int32, (128, 128), 1)
    shift = jnp.where(row == lane, 0.1, 0.0)
    share = 1.0 / 32768.0

    def put(i, j, value):
        value = value * share
        mats[which, i * 128:i * 128 + 128, j * 128:j * 128 + 128] = value + shift if i == j else value

    for i in range(2):
        for j in range(2):
            low = large[j * HALF + i * 128:j * HALF + i * 128 + 128, :]
            put(i, j, small[j * HALF + i * 128:j * HALF + i * 128 + 128, :])
            put(2 + i, j, low)
            put(j, 2 + i, low.T)
            put(2 + i, 2 + j, large[WIDTH + j * HALF + i * 128:WIDTH + j * HALF + i * 128 + 128, :])


def invert(mats, beside):
    wide_lane = lax.broadcasted_iota(jnp.int32, (64, WIDTH), 1)
    wide_row = lax.broadcasted_iota(jnp.int32, (64, WIDTH), 0)

    def eliminate(block, carry):
        for odd in range(2):
            for b in range(4):
                pl.when(block == b)(functools.partial(beside, 2 * b + odd))
            at = pl.multiple_of(block * 128 + odd * 64, 64)
            rows = pl.ds(at, 64)
            pair = []
            for which in range(2):
                square = mats[which, rows, pl.ds(pl.multiple_of(block * 128, 128), 128)]
                pair.append(square[:, odd * 64:odd * 64 + 64])
            both = jnp.concatenate(pair, axis=1)
            done = jnp.concatenate(sweep_pair([both[8 * i:8 * i + 8] for i in range(8)]), axis=0)
            in_block = (wide_lane >= at) & (wide_lane < at + 64)
            for which in range(2):
                panel = mats[which, rows, :]
                top = jnp.where(in_block, jnp.where(wide_lane - at == wide_row, 1.0, 0.0), -panel)
                fresh = product(done[:, which * 64:which * 64 + 64], top, (1, 0), (1, 0))
                for part in range(2):
                    half = pl.ds(part * 256, 256)
                    step = product(panel[:, part * 256:part * 256 + 256], fresh, (0, 0), (0, 0))
                    mats[which, half, :] = jnp.where(in_block[:1], 0.0, mats[which, half, :]) - step
                mats[which, rows, :] = fresh
        return carry

    lax.fori_loop(0, 4, eliminate, 0)


def packed(ref):
    return jnp.concatenate([ref[i * HALF:i * HALF + HALF, :] for i in range(4)], axis=1)


def kernel(act_ref, cot_ref, w_ref, out_ref, w_buf, xs, slopes, scales, grads, u_own, dh_own, mats, p_mat, *rest):
    gather_refs, sems, stream_refs = rest[:9], rest[9], rest[10:]
    rank = lax.axis_index("dp")
    streams = []
    for i in range(6):
        streams.append(Stream(i, stream_refs[9 * i:9 * i + 9], sems, i % 2 == 1))
    a_small, a_large, g_small, g_large, d_top, d_low = streams

    xs[0] = act_ref[...]
    grads[...] = cot_ref[...]
    gather_weights(w_ref, w_buf, *gather_refs)
    run_ahead(w_buf, xs, slopes, scales, u_own)

    def factor(ref, small, large):
        keep(small.part, 0, dot(ref[:, :HALF], ref[:, :HALF], (0, 0)))
        keep(large.part, 0, dot(ref[:, HALF:], ref[:, :HALF], (0, 0)))
        keep(large.part, WIDTH, dot(ref[:, HALF:], ref[:, HALF:], (0, 0)))

    def advance(group, t):
        for stream in group:
            stream.advance(t)

    in_pair, out_pair, d_pair = streams[:2], streams[2:4], streams[4:]
    factor(u_own, a_small, a_large)
    advance(in_pair, 0)

    def beside_back(step):
        for t in range(1, 5):
            pl.when(step == 2 * t - 1)(functools.partial(advance, in_pair, t))

    run_back(w_buf, xs, slopes, scales, grads, dh_own, beside_back)
    factor(dh_own, g_small, g_large)
    advance(out_pair, 0)
    keep(d_top.part, 0, dot(u_own[:, :HALF], dh_own[...], (0, 0)))
    keep(d_low.part, 0, dot(u_own[:, HALF:], dh_own[...], (0, 0)))
    for t in range(1, 13):
        advance(out_pair, t)
        if t + 4 <= 12:
            advance(in_pair, t + 4)
        if t + 4 == 12:
            load_factor(mats, 0, a_small.full, a_large.full)
        if t >= 8:
            advance(d_pair, t - 8)
    load_factor(mats, 1, g_small.full, g_large.full)

    def beside_invert(step):
        advance(d_pair, 5 + step)

    invert(mats, beside_invert)
    d_mat = jnp.concatenate([packed(d_top.full), packed(d_low.full)], axis=0)
    p_mat[...] = product(mats[0], d_mat, (1, 0), (1, 0))
    p_mat[...] = product(p_mat[...], mats[1], (1, 0), (1, 0))
    whole = p_mat[...]
    mean = jnp.sum(jnp.sum(whole * whole, axis=0, keepdims=True), axis=1, keepdims=True) * (1.0 / (WIDTH * WIDTH))
    mine = p_mat[pl.ds(pl.multiple_of(rank * 8, 8), 8), :]
    out_ref[...] = mine / jnp.sqrt(mean + 1e-06)
    for stream in streams:
        stream.close()


def local(first_acts, cotangent, weights):
    square = lambda n, kind: pltpu.VMEM((n, TOKENS, WIDTH), kind)
    flat = lambda kind: pltpu.VMEM((TOKENS, WIDTH), kind)
    copies = pltpu.SemaphoreType.DMA
    scratch = [
        pltpu.VMEM((2, 4, 2, 4, 128, HALF), jnp.bfloat16),
        square(LAYERS + 1, jnp.bfloat16),
        square(LAYERS, jnp.float32),
        pltpu.VMEM((LAYERS, TOKENS, 128), jnp.float32),
        flat(jnp.bfloat16), flat(jnp.bfloat16), flat(jnp.bfloat16),
        square(2, jnp.float32), flat(jnp.float32),
        pltpu.VMEM((8, HALF), jnp.float32),
        pltpu.VMEM((8, HALF), jnp.float32),
        copies((2,)), copies((16,)), copies((16,)),
        copies((4, 16)), copies((4, 16)), copies((4, 16)), copies((4, 16)),
        copies((2, 6, 12)),
    ]
    for rows in (512, 1024, 512, 1024, 1024, 1024):
        sizes = [rows, rows // 2, rows] + [rows // 2 >> t for t in range(6)]
        scratch += [pltpu.VMEM((size, 128), jnp.float32) for size in sizes]
    return pl.pallas_call(
        kernel,
        out_shape=jax.ShapeDtypeStruct((8, WIDTH), jnp.float32),
        in_specs=[pl.BlockSpec(memory_space=pltpu.VMEM)] * 3,
        out_specs=pl.BlockSpec(memory_space=pltpu.VMEM),
        scratch_shapes=scratch,
        compiler_params=pltpu.CompilerParams(
            collective_id=0, has_side_effects=True, vmem_limit_bytes=VMEM_LIMIT
        ),
        name="chain_and_factors",
    )(first_acts.reshape(TOKENS, WIDTH), cotangent.reshape(TOKENS, WIDTH), weights)


def solution(mesh):
    placed = (P(None, "dp", None), P(None, "dp", None), P(("section", "dp"), None))
    return jax.shard_map(
        local, mesh=mesh, in_specs=placed, out_specs=P(("section", "dp"), None), check_vma=False
    )
```

```python
import functools

import jax
import jax.numpy as jnp
from jax import lax
from jax.experimental import pallas as pl
from jax.experimental.pallas import tpu as pltpu
from jax.sharding import PartitionSpec as P

MESH = pl.DeviceIdType.MESH
WIDTH = 512
TOKENS = 512
LAYERS = 8
HALF = 256
VMEM_LIMIT = 56 * 1024 * 1024


def place():
    section = lax.axis_index("section")
    rank = lax.axis_index("dp")
    y, z_hi = section // 2, section % 2
    x, z_lo, core = rank // 16, (rank % 16) // 2, rank % 2
    return x, y, z_hi, z_lo, core


def device(x, y, z_hi, z_lo, core):
    return (y * 2 + z_hi, x * 16 + z_lo * 2 + core)


def flip_low(v):
    return v + 1 - 2 * (v % 2)


def send(src, dst, send_sem, recv_sem, target):
    copy = pltpu.make_async_remote_copy(
        src_ref=src, dst_ref=dst, send_sem=send_sem, recv_sem=recv_sem,
        device_id=target, device_id_type=MESH,
    )
    copy.start()
    return copy


def meet(targets):
    barrier = pltpu.get_barrier_semaphore()
    for target in targets:
        pl.semaphore_signal(barrier, inc=1, device_id=target, device_id_type=MESH)
    pl.semaphore_wait(barrier, len(targets))


def gather_weights(w_ref, buf, mine_ref, sib_ref, sib_sem, z_send, z_recv, h_send, h_recv, c_send, c_recv):
    x, y, z_hi, z_lo, core = place()
    z = z_hi * 8 + z_lo
    sibling = device(x, y, z_hi, z_lo, 1 - core)
    z_peers = []
    for k in range(1, 16):
        other = (z + k) % 16
        z_peers.append(device(x, y, other // 8, other % 8, core))
    moves = [
        (lambda a, b: (flip_low(a), b)),
        (lambda a, b: (3 - a, b)),
        (lambda a, b: (a, flip_low(b))),
        (lambda a, b: (a, 3 - b)),
    ]
    orders = [(0, 1, 2, 3), (1, 2, 3, 0), (2, 3, 0, 1), (3, 0, 1, 2)]
    partners = []
    for move in moves:
        px, py = move(x, y)
        partners.append(device(px, py, z_hi, z_lo, core))
    meet([sibling] + z_peers + partners)

    first = core == 0
    wf = w_ref[...].astype(jnp.float32)
    left, right = wf[:, :256], wf[:, 256:]
    mine_ref[...] = jnp.where(first, right, left)
    swap = send(mine_ref, sib_ref, sib_sem.at[0], sib_sem.at[1], sibling)
    mine = jnp.where(first, left, right)
    swap.wait()
    theirs = sib_ref[...]
    rows = jnp.concatenate([jnp.where(first, mine, theirs), jnp.where(first, theirs, mine)], axis=0)
    own = buf.at[core, y, z_hi, x, pl.ds(pl.multiple_of(z_lo * 16, 16), 16), :]
    own[...] = rows.astype(jnp.bfloat16)
    z_copies = [send(own, own, z_send.at[k], z_recv.at[k], z_peers[k - 1]) for k in range(1, 16)]
    for copy in z_copies:
        copy.wait_recv()

    def block(j, at):
        bx, by = at
        return buf.at[core, by, j // 2, bx, pl.ds((j % 2) * 64, 64), :]

    held = {}
    copies = {}
    across = {}

    def forward(j, r, step_from):
        ref = block(j, held[j, r])
        for step in range(step_from, 4):
            index = 2 ** step + r
            copies[j, index] = send(
                ref, ref, h_send.at[j, index], h_recv.at[j, index], partners[orders[j][step]]
            )
        across[j, r] = send(ref, ref, c_send.at[j, r], c_recv.at[j, r], sibling)

    for j in range(4):
        held[j, 0] = (x, y)
        for r in range(1, 16):
            step = r.bit_length() - 1
            held[j, r] = moves[orders[j][step]](*held[j, r - 2 ** step])
    for j in range(4):
        forward(j, 0, 0)
    arrivals = sorted(range(1, 16), key=lambda r: (bin(r).count("1"), r))
    for r in arrivals:
        for j in range(4):
            copies[j, r].wait_recv()
            forward(j, r, r.bit_length())
    for j in range(4):
        for r in range(16):
            across[j, r].wait_recv()
    for copy in z_copies:
        copy.wait_send()
    for j in range(4):
        for r in range(16):
            across[j, r].wait_send()
            if r:
                copies[j, r].wait_send()


def gelu_parts(h):
    coeff = 0.7978845608028654
    inner = coeff * (h + 0.044715 * h * h * h)
    tanh_val = jnp.tanh(inner)
    value = 0.5 * h * (1.0 + tanh_val)
    slope = 0.5 * (1.0 + tanh_val) + 0.5 * h * (1.0 - tanh_val * tanh_val) * coeff * (
        1.0 + 3.0 * 0.044715 * h * h
    )
    return (value, slope)


def dot(a, b, dims):
    return lax.dot_general(
        a, b, ((dims[:1], dims[1:]), ((), ())), preferred_element_type=jnp.float32
    )


def splat(value):
    return jnp.broadcast_to(value, (8, 128))


def thirds(value):
    high = value.astype(jnp.bfloat16).astype(jnp.float32)
    rest = value - high
    middle = rest.astype(jnp.bfloat16).astype(jnp.float32)
    return high, middle, rest - middle


def product(a, b, dims, axes):
    a0, a1, a2 = thirds(a)
    b0, b1, b2 = thirds(b)
    long_a = jnp.concatenate([a0, a0, a1, a1, a0, a2], axis=axes[0]).astype(jnp.bfloat16)
    long_b = jnp.concatenate([b0, b1, b0, b1, b2, b0], axis=axes[1]).astype(jnp.bfloat16)
    return dot(long_a, long_b, dims)


def minus_inverse(e):
    at = lambda i, k: (min(i, k), max(i, k))
    for k in range(0, 8, 2):
        a, b, c = e[k, k], e[k, k + 1], e[k + 1, k + 1]
        scale = 1.0 / (a * c - b * b)
        ia, ib, ic = c * scale, -(b * scale), a * scale
        others = [i for i in range(8) if i not in (k, k + 1)]
        r0 = {i: ia * e[at(i, k)] + ib * e[at(i, k + 1)] for i in others}
        r1 = {i: ib * e[at(i, k)] + ic * e[at(i, k + 1)] for i in others}
        for i in others:
            for j in others:
                if i <= j:
                    e[i, j] = e[i, j] - (e[at(i, k)] * r0[j] + e[at(i, k + 1)] * r1[j])
        for i in others:
            e[at(i, k)], e[at(i, k + 1)] = r0[i], r1[i]
        e[k, k], e[k, k + 1], e[k + 1, k + 1] = -ia, -ib, -ic
    return lambda i, k: e[at(i, k)]


def sweep_pair(tiles):
    tiles = list(tiles)
    lane = lax.broadcasted_iota(jnp.int32, (8, 128), 1)
    row = lax.broadcasted_iota(jnp.int32, (8, 128), 0)
    first = lane < 64
    local_lane = lane % 64

    def column(tile, k):
        return jnp.where(first, splat(tile[:, k:k + 1]), splat(tile[:, 64 + k:65 + k]))

    for p in range(8):
        pivot = tiles[p]
        base = 8 * p
        in_block = (local_lane >= base) & (local_lane < base + 8)
        columns = [column(pivot, base + k) for k in range(8)]
        e = {}
        for k in range(8):
            for i in range(k + 1):
                e[i, k] = splat(columns[k][i:i + 1, :])
        inverse = minus_inverse(e)
        top = jnp.where(in_block, jnp.where(local_lane - base == row, 1.0, 0.0), -pivot)
        result = None
        for k in range(8):
            spread = inverse(0, k)
            for i in range(1, 8):
                spread = jnp.where(row == i, inverse(i, k), spread)
            term = spread * splat(top[k:k + 1, :])
            result = term if result is None else result + term
        tiles[p] = result
        if p < 7:
            value = jnp.where(in_block, 0.0, tiles[p + 1])
            for k in range(8):
                value = value - column(tiles[p + 1], base + k) * splat(result[k:k + 1, :])
        update = product(pivot, result, (0, 0), (0, 0))
        for i in range(8):
            if i not in (p, p + 1):
                step = jnp.where(first, update[8 * i:8 * i + 8], update[64 + 8 * i:72 + 8 * i])
                tiles[i] = jnp.where(in_block, 0.0, tiles[i]) - step
        if p < 7:
            tiles[p + 1] = value
    return tiles


def run_ahead(w_buf, xs, slopes, scales, u_own):
    section = lax.axis_index("section")

    def ahead(layer, carry):
        xf = xs[layer].astype(jnp.float32)
        scale = lax.rsqrt(jnp.mean(xf * xf, axis=-1, keepdims=True) + 1e-05)
        scales[layer] = jnp.broadcast_to(scale, (TOKENS, 128))
        unit = (xf * scale).astype(jnp.bfloat16)

        @pl.when(layer == section)
        def _():
            u_own[...] = unit

        for half in range(2):
            columns = slice(half * HALF, half * HALF + HALF)
            w_half = w_buf[half, layer // 2, layer % 2].reshape(WIDTH, HALF)
            value, slope = gelu_parts(dot(unit, w_half, (1, 0)))
            slopes[layer, :, columns] = slope
            xs[layer + 1, :, columns] = (xf[:, columns] + value).astype(jnp.bfloat16)
        return carry

    lax.fori_loop(0, LAYERS, ahead, 0)


def run_back(w_buf, xs, slopes, scales, grads, dh_own, beside):
    section = lax.axis_index("section")

    def back(step, carry):
        beside(step)
        layer = LAYERS - 1 - step
        grad = grads[...].astype(jnp.float32)
        d_h = (grad * slopes[layer]).astype(jnp.bfloat16)

        @pl.when(layer == section)
        def _():
            dh_own[...] = d_h

        d_u = None
        for half in range(2):
            w_half = w_buf[half, layer // 2, layer % 2].reshape(WIDTH, HALF)
            term = dot(d_h[:, half * HALF:half * HALF + HALF], w_half, (1, 1))
            d_u = term if d_u is None else d_u + term
        xf = xs[layer].astype(jnp.float32)
        scale = scales[layer, :, 0:1]
        shift = scale * scale * scale * jnp.mean(d_u * xf, axis=-1, keepdims=True)
        grads[...] = (grad + (scale * d_u - xf * shift)).astype(jnp.bfloat16)
        return carry

    lax.fori_loop(0, LAYERS - 1, back, 0)

    @pl.when(section == 0)
    def _():
        dh_own[...] = (grads[...].astype(jnp.float32) * slopes[0]).astype(jnp.bfloat16)


def keep(ref, at, value):
    for i in range(value.shape[1] // 128):
        ref[at + i * HALF:at + i * HALF + HALF, :] = value[:, i * 128:i * 128 + 128]


class Stream:
    LAST = 8

    def __init__(self, index, refs, sems, z_sems, swap_x):
        self.part, self.acc, self.full, self.got_core, self.got_one, self.got_two, self.got_z = refs
        self.sems, self.z_sems, self.index = sems, z_sems, index
        self.half = self.part.shape[0] // 2
        self.chunk = self.half // 32
        x, y, z_hi, z_lo, core = place()
        self.core, self.z_lo = core, z_lo
        self.sibling = device(x, y, z_hi, z_lo, 1 - core)
        steps = [
            (((x + 1) // 2) % 2, device(flip_low(x), y, z_hi, z_lo, core)),
            (x // 2, device(3 - x, y, z_hi, z_lo, core)),
        ]
        if swap_x:
            steps.reverse()
        base = 0
        self.sent, self.kept, self.peers = [0], [0], [self.sibling]
        for t, (bit, peer) in enumerate(steps, 1):
            size = self.half >> t
            self.sent.append(base + (1 - bit) * size)
            base = base + bit * size
            self.kept.append(base)
            self.peers.append(peer)
        self.z_peers = [device(x, y, z_hi, (z_lo + k) % 8, core) for k in range(8)]

    def span(self, at, size):
        return pl.ds(pl.multiple_of(at, 8), size)

    def copy(self, t):
        half = self.half
        if t == 0:
            src, dst, peer = self.part.at[self.span((1 - self.core) * half, half)], self.got_core, self.sibling
        elif t <= 2:
            src, peer = self.acc.at[self.span(self.sent[t], half >> t)], self.peers[t]
            dst = self.got_one if t == 1 else self.got_two
        else:
            k = 7 - t
            src = self.full.at[self.span(self.core * half + self.kept[k], half >> k)]
            dst, peer = src, self.peers[k]
        return pltpu.make_async_remote_copy(
            src_ref=src, dst_ref=dst, send_sem=self.sems.at[0, self.index, t],
            recv_sem=self.sems.at[1, self.index, t], device_id=peer, device_id_type=MESH,
        )

    def summed(self, z_lo):
        return self.span(self.core * self.half + self.kept[2] + z_lo * self.chunk, self.chunk)

    def z_copy(self, t, k, arriving=False):
        if t == 3:
            there = (self.z_lo + k) % 8
            src = self.acc.at[self.span(self.kept[2] + there * self.chunk, self.chunk)]
            dst = self.got_z.at[k - 1]
        else:
            src = self.full.at[self.summed((self.z_lo + 8 - k) % 8 if arriving else self.z_lo)]
            dst = src
        return pltpu.make_async_remote_copy(
            src_ref=src, dst_ref=dst, send_sem=self.z_sems.at[0, t - 3, self.index, k],
            recv_sem=self.z_sems.at[1, t - 3, self.index, k], device_id=self.z_peers[k], device_id_type=MESH,
        )

    def advance(self, t):
        if t > 0:
            done = t - 1
            if done in (3, 4):
                for k in range(1, 8):
                    self.z_copy(done, k, True).wait_recv()
            else:
                self.copy(done).wait_recv()
            if done == 0:
                self.acc[...] = self.part[self.span(self.core * self.half, self.half), :] + self.got_core[...]
            elif done <= 2:
                mine = self.span(self.kept[done], self.half >> done)
                got = self.got_one if done == 1 else self.got_two
                self.acc[mine, :] = self.acc[mine, :] + got[...]
            elif done == 3:
                total = self.acc[self.span(self.kept[2] + self.z_lo * self.chunk, self.chunk), :]
                for k in range(7):
                    total = total + self.got_z[k]
                self.full[self.summed(self.z_lo), :] = total
        if t in (3, 4):
            for k in (4, 3, 5, 2, 6, 1, 7):
                self.z_copy(t, k).start()
        elif t < 8:
            self.copy(t).start()

    def close(self):
        for t in range(8):
            if t in (3, 4):
                for k in range(1, 8):
                    self.z_copy(t, k).wait_send()
            else:
                self.copy(t).wait_send()


def load_factor(mats, which, small, large):
    row = lax.broadcasted_iota(jnp.int32, (128, 128), 0)
    lane = lax.broadcasted_iota(jnp.int32, (128, 128), 1)
    shift = jnp.where(row == lane, 0.1, 0.0)
    share = 1.0 / 32768.0

    def put(i, j, value):
        value = value * share
        mats[which, i * 128:i * 128 + 128, j * 128:j * 128 + 128] = value + shift if i == j else value

    for i in range(2):
        for j in range(2):
            low = large[j * HALF + i * 128:j * HALF + i * 128 + 128, :]
            put(i, j, small[j * HALF + i * 128:j * HALF + i * 128 + 128, :])
            put(2 + i, j, low)
            put(j, 2 + i, low.T)
            put(2 + i, 2 + j, large[WIDTH + j * HALF + i * 128:WIDTH + j * HALF + i * 128 + 128, :])


def invert(mats, beside):
    wide_lane = lax.broadcasted_iota(jnp.int32, (64, WIDTH), 1)
    wide_row = lax.broadcasted_iota(jnp.int32, (64, WIDTH), 0)

    def eliminate(block, carry):
        for odd in range(2):
            for b in range(4):
                pl.when(block == b)(functools.partial(beside, 2 * b + odd))
            at = pl.multiple_of(block * 128 + odd * 64, 64)
            rows = pl.ds(at, 64)
            pair = []
            for which in range(2):
                square = mats[which, rows, pl.ds(pl.multiple_of(block * 128, 128), 128)]
                pair.append(square[:, odd * 64:odd * 64 + 64])
            both = jnp.concatenate(pair, axis=1)
            done = jnp.concatenate(sweep_pair([both[8 * i:8 * i + 8] for i in range(8)]), axis=0)
            in_block = (wide_lane >= at) & (wide_lane < at + 64)
            for which in range(2):
                panel = mats[which, rows, :]
                top = jnp.where(in_block, jnp.where(wide_lane - at == wide_row, 1.0, 0.0), -panel)
                fresh = product(done[:, which * 64:which * 64 + 64], top, (1, 0), (1, 0))
                for part in range(2):
                    half = pl.ds(part * 256, 256)
                    step = product(panel[:, part * 256:part * 256 + 256], fresh, (0, 0), (0, 0))
                    mats[which, half, :] = jnp.where(in_block[:1], 0.0, mats[which, half, :]) - step
                mats[which, rows, :] = fresh
        return carry

    lax.fori_loop(0, 4, eliminate, 0)


def packed(ref):
    return jnp.concatenate([ref[i * HALF:i * HALF + HALF, :] for i in range(4)], axis=1)


def kernel(act_ref, cot_ref, w_ref, out_ref, w_buf, xs, slopes, scales, grads, u_own, dh_own, mats, p_mat, *rest):
    gather_refs, sems, z_sems, stream_refs = rest[:9], rest[9], rest[10], rest[11:]
    rank = lax.axis_index("dp")
    streams = []
    for i in range(6):
        streams.append(Stream(i, stream_refs[7 * i:7 * i + 7], sems, z_sems, i % 2 == 1))
    a_small, a_large, g_small, g_large, d_top, d_low = streams

    xs[0] = act_ref[...]
    grads[...] = cot_ref[...]
    gather_weights(w_ref, w_buf, *gather_refs)
    run_ahead(w_buf, xs, slopes, scales, u_own)

    def factor(ref, small, large):
        keep(small.part, 0, dot(ref[:, :HALF], ref[:, :HALF], (0, 0)))
        keep(large.part, 0, dot(ref[:, HALF:], ref[:, :HALF], (0, 0)))
        keep(large.part, WIDTH, dot(ref[:, HALF:], ref[:, HALF:], (0, 0)))

    def advance(group, t):
        for stream in group:
            stream.advance(t)

    in_pair, out_pair, d_pair = streams[:2], streams[2:4], streams[4:]
    factor(u_own, a_small, a_large)
    advance(in_pair, 0)

    def beside_back(step):
        for t, at in ((1, 2), (2, 4), (3, 6)):
            pl.when(step == at)(functools.partial(advance, in_pair, t))

    run_back(w_buf, xs, slopes, scales, grads, dh_own, beside_back)
    factor(dh_own, g_small, g_large)
    advance(out_pair, 0)
    keep(d_top.part, 0, dot(u_own[:, :HALF], dh_own[...], (0, 0)))
    keep(d_low.part, 0, dot(u_own[:, HALF:], dh_own[...], (0, 0)))
    for t in range(1, 9):
        advance(out_pair, t)
        if t + 3 <= 8:
            advance(in_pair, t + 3)
        if t + 3 == 8:
            load_factor(mats, 0, a_small.full, a_large.full)
        if t >= 2:
            advance(d_pair, t - 2)
    load_factor(mats, 1, g_small.full, g_large.full)

    def beside_invert(step):
        if step in (2, 4):
            advance(d_pair, 6 + step // 2)

    invert(mats, beside_invert)
    d_mat = jnp.concatenate([packed(d_top.full), packed(d_low.full)], axis=0)
    p_mat[...] = product(mats[0], d_mat, (1, 0), (1, 0))
    p_mat[...] = product(p_mat[...], mats[1], (1, 0), (1, 0))
    whole = p_mat[...]
    mean = jnp.sum(jnp.sum(whole * whole, axis=0, keepdims=True), axis=1, keepdims=True) * (1.0 / (WIDTH * WIDTH))
    mine = p_mat[pl.ds(pl.multiple_of(rank * 8, 8), 8), :]
    out_ref[...] = mine / jnp.sqrt(mean + 1e-06)
    for stream in streams:
        stream.close()


def local(first_acts, cotangent, weights):
    square = lambda n, kind: pltpu.VMEM((n, TOKENS, WIDTH), kind)
    flat = lambda kind: pltpu.VMEM((TOKENS, WIDTH), kind)
    copies = pltpu.SemaphoreType.DMA
    scratch = [
        pltpu.VMEM((2, 4, 2, 4, 128, HALF), jnp.bfloat16),
        square(LAYERS + 1, jnp.bfloat16),
        square(LAYERS, jnp.float32),
        pltpu.VMEM((LAYERS, TOKENS, 128), jnp.float32),
        flat(jnp.bfloat16), flat(jnp.bfloat16), flat(jnp.bfloat16),
        square(2, jnp.float32), flat(jnp.float32),
        pltpu.VMEM((8, HALF), jnp.float32),
        pltpu.VMEM((8, HALF), jnp.float32),
        copies((2,)), copies((16,)), copies((16,)),
        copies((4, 16)), copies((4, 16)), copies((4, 16)), copies((4, 16)),
        copies((2, 6, 8)), copies((2, 2, 6, 8)),
    ]
    for rows in (512, 1024, 512, 1024, 1024, 1024):
        sizes = [rows, rows // 2, rows, rows // 2, rows // 4, rows // 8]
        scratch += [pltpu.VMEM((size, 128), jnp.float32) for size in sizes]
        scratch.append(pltpu.VMEM((7, rows // 64, 128), jnp.float32))
    return pl.pallas_call(
        kernel,
        out_shape=jax.ShapeDtypeStruct((8, WIDTH), jnp.float32),
        in_specs=[pl.BlockSpec(memory_space=pltpu.VMEM)] * 3,
        out_specs=pl.BlockSpec(memory_space=pltpu.VMEM),
        scratch_shapes=scratch,
        compiler_params=pltpu.CompilerParams(
            collective_id=0, has_side_effects=True, vmem_limit_bytes=VMEM_LIMIT
        ),
        name="chain_and_factors",
    )(first_acts.reshape(TOKENS, WIDTH), cotangent.reshape(TOKENS, WIDTH), weights)


def solution(mesh):
    placed = (P(None, "dp", None), P(None, "dp", None), P(("section", "dp"), None))
    return jax.shard_map(
        local, mesh=mesh, in_specs=placed, out_specs=P(("section", "dp"), None), check_vma=False
    )
```

```python
import functools

import jax
import jax.numpy as jnp
from jax import lax
from jax.experimental import pallas as pl
from jax.experimental.pallas import tpu as pltpu
from jax.sharding import PartitionSpec as P

MESH = pl.DeviceIdType.MESH
WIDTH = 512
TOKENS = 512
LAYERS = 8
HALF = 256
VMEM_LIMIT = 56 * 1024 * 1024


def place():
    section = lax.axis_index("section")
    rank = lax.axis_index("dp")
    y, z_hi = section // 2, section % 2
    x, z_lo, core = rank // 16, (rank % 16) // 2, rank % 2
    return x, y, z_hi, z_lo, core


def device(x, y, z_hi, z_lo, core):
    return (y * 2 + z_hi, x * 16 + z_lo * 2 + core)


def flip_low(v):
    return v + 1 - 2 * (v % 2)


def send(src, dst, send_sem, recv_sem, target):
    copy = pltpu.make_async_remote_copy(
        src_ref=src, dst_ref=dst, send_sem=send_sem, recv_sem=recv_sem,
        device_id=target, device_id_type=MESH,
    )
    copy.start()
    return copy


def meet(targets):
    barrier = pltpu.get_barrier_semaphore()
    for target in targets:
        pl.semaphore_signal(barrier, inc=1, device_id=target, device_id_type=MESH)
    pl.semaphore_wait(barrier, len(targets))


def gather_weights(w_ref, buf, mine_ref, sib_ref, sib_sem, z_send, z_recv, h_send, h_recv, c_send, c_recv):
    x, y, z_hi, z_lo, core = place()
    z = z_hi * 8 + z_lo
    sibling = device(x, y, z_hi, z_lo, 1 - core)
    z_peers = []
    for k in range(1, 16):
        other = (z + k) % 16
        z_peers.append(device(x, y, other // 8, other % 8, core))
    moves = [
        (lambda a, b: (flip_low(a), b)),
        (lambda a, b: (3 - a, b)),
        (lambda a, b: (a, flip_low(b))),
        (lambda a, b: (a, 3 - b)),
    ]
    orders = [(0, 1, 2, 3), (1, 2, 3, 0), (2, 3, 0, 1), (3, 0, 1, 2)]
    partners = []
    for move in moves:
        px, py = move(x, y)
        partners.append(device(px, py, z_hi, z_lo, core))
    meet([sibling] + z_peers + partners + [device((x + 2) % 4, y, z_hi, z_lo, core)])

    first = core == 0
    wf = w_ref[...].astype(jnp.float32)
    left, right = wf[:, :256], wf[:, 256:]
    mine_ref[...] = jnp.where(first, right, left)
    swap = send(mine_ref, sib_ref, sib_sem.at[0], sib_sem.at[1], sibling)
    mine = jnp.where(first, left, right)
    swap.wait()
    theirs = sib_ref[...]
    rows = jnp.concatenate([jnp.where(first, mine, theirs), jnp.where(first, theirs, mine)], axis=0)
    own = buf.at[core, y, z_hi, x, pl.ds(pl.multiple_of(z_lo * 16, 16), 16), :]
    own[...] = rows.astype(jnp.bfloat16)
    z_copies = [send(own, own, z_send.at[k], z_recv.at[k], z_peers[k - 1]) for k in range(1, 16)]
    for copy in z_copies:
        copy.wait_recv()

    def block(j, at):
        bx, by = at
        return buf.at[core, by, j // 2, bx, pl.ds((j % 2) * 64, 64), :]

    held = {}
    copies = {}
    across = {}

    def forward(j, r, step_from):
        ref = block(j, held[j, r])
        for step in range(step_from, 4):
            index = 2 ** step + r
            copies[j, index] = send(
                ref, ref, h_send.at[j, index], h_recv.at[j, index], partners[orders[j][step]]
            )
        across[j, r] = send(ref, ref, c_send.at[j, r], c_recv.at[j, r], sibling)

    for j in range(4):
        held[j, 0] = (x, y)
        for r in range(1, 16):
            step = r.bit_length() - 1
            held[j, r] = moves[orders[j][step]](*held[j, r - 2 ** step])
    for j in range(4):
        forward(j, 0, 0)
    arrivals = sorted(range(1, 16), key=lambda r: (bin(r).count("1"), r))
    for r in arrivals:
        for j in range(4):
            copies[j, r].wait_recv()
            forward(j, r, r.bit_length())
    for j in range(4):
        for r in range(16):
            across[j, r].wait_recv()
    for copy in z_copies:
        copy.wait_send()
    for j in range(4):
        for r in range(16):
            across[j, r].wait_send()
            if r:
                copies[j, r].wait_send()


def gelu_parts(h):
    coeff = 0.7978845608028654
    inner = coeff * (h + 0.044715 * h * h * h)
    tanh_val = jnp.tanh(inner)
    value = 0.5 * h * (1.0 + tanh_val)
    slope = 0.5 * (1.0 + tanh_val) + 0.5 * h * (1.0 - tanh_val * tanh_val) * coeff * (
        1.0 + 3.0 * 0.044715 * h * h
    )
    return (value, slope)


def dot(a, b, dims):
    return lax.dot_general(
        a, b, ((dims[:1], dims[1:]), ((), ())), preferred_element_type=jnp.float32
    )


def splat(value):
    return jnp.broadcast_to(value, (8, 128))


def thirds(value):
    high = value.astype(jnp.bfloat16).astype(jnp.float32)
    rest = value - high
    middle = rest.astype(jnp.bfloat16).astype(jnp.float32)
    return high, middle, rest - middle


def product(a, b, dims, axes):
    a0, a1, a2 = thirds(a)
    b0, b1, b2 = thirds(b)
    long_a = jnp.concatenate([a0, a0, a1, a1, a0, a2], axis=axes[0]).astype(jnp.bfloat16)
    long_b = jnp.concatenate([b0, b1, b0, b1, b2, b0], axis=axes[1]).astype(jnp.bfloat16)
    return dot(long_a, long_b, dims)


def halves(value):
    high = value.astype(jnp.bfloat16)
    return high, (value - high.astype(jnp.float32)).astype(jnp.bfloat16)


def product_of_halves(a, b):
    a0, a1 = halves(a)
    b0, b1 = halves(b)
    return dot(a0, b0, (1, 0)) + (dot(a0, b1, (1, 0)) + dot(a1, b0, (1, 0)))


def minus_inverse(e):
    at = lambda i, k: (min(i, k), max(i, k))
    for k in range(0, 8, 2):
        a, b, c = e[k, k], e[k, k + 1], e[k + 1, k + 1]
        scale = 1.0 / (a * c - b * b)
        ia, ib, ic = c * scale, -(b * scale), a * scale
        others = [i for i in range(8) if i not in (k, k + 1)]
        r0 = {i: ia * e[at(i, k)] + ib * e[at(i, k + 1)] for i in others}
        r1 = {i: ib * e[at(i, k)] + ic * e[at(i, k + 1)] for i in others}
        for i in others:
            for j in others:
                if i <= j:
                    e[i, j] = e[i, j] - (e[at(i, k)] * r0[j] + e[at(i, k + 1)] * r1[j])
        for i in others:
            e[at(i, k)], e[at(i, k + 1)] = r0[i], r1[i]
        e[k, k], e[k, k + 1], e[k + 1, k + 1] = -ia, -ib, -ic
    return lambda i, k: e[at(i, k)]


def sweep_pair(tiles):
    tiles = list(tiles)
    lane = lax.broadcasted_iota(jnp.int32, (8, 128), 1)
    row = lax.broadcasted_iota(jnp.int32, (8, 128), 0)
    first = lane < 64
    local_lane = lane % 64

    def column(tile, k):
        return jnp.where(first, splat(tile[:, k:k + 1]), splat(tile[:, 64 + k:65 + k]))

    for p in range(8):
        pivot = tiles[p]
        base = 8 * p
        in_block = (local_lane >= base) & (local_lane < base + 8)
        columns = [column(pivot, base + k) for k in range(8)]
        e = {}
        for k in range(8):
            for i in range(k + 1):
                e[i, k] = splat(columns[k][i:i + 1, :])
        inverse = minus_inverse(e)
        top = jnp.where(in_block, jnp.where(local_lane - base == row, 1.0, 0.0), -pivot)
        result = None
        for k in range(8):
            spread = inverse(0, k)
            for i in range(1, 8):
                spread = jnp.where(row == i, inverse(i, k), spread)
            term = spread * splat(top[k:k + 1, :])
            result = term if result is None else result + term
        tiles[p] = result
        if p < 7:
            value = jnp.where(in_block, 0.0, tiles[p + 1])
            for k in range(8):
                value = value - column(tiles[p + 1], base + k) * splat(result[k:k + 1, :])
        update = product(pivot, result, (0, 0), (0, 0))
        for i in range(8):
            if i not in (p, p + 1):
                step = jnp.where(first, update[8 * i:8 * i + 8], update[64 + 8 * i:72 + 8 * i])
                tiles[i] = jnp.where(in_block, 0.0, tiles[i]) - step
        if p < 7:
            tiles[p + 1] = value
    return tiles


def run_ahead(w_buf, xs, slopes, scales, u_own):
    section = lax.axis_index("section")

    def ahead(layer, carry):
        xf = xs[layer].astype(jnp.float32)
        scale = lax.rsqrt(jnp.mean(xf * xf, axis=-1, keepdims=True) + 1e-05)
        scales[layer] = jnp.broadcast_to(scale, (TOKENS, 128))
        unit = (xf * scale).astype(jnp.bfloat16)

        @pl.when(layer == section)
        def _():
            u_own[...] = unit

        for half in range(2):
            columns = slice(half * HALF, half * HALF + HALF)
            w_half = w_buf[half, layer // 2, layer % 2].reshape(WIDTH, HALF)
            value, slope = gelu_parts(dot(unit, w_half, (1, 0)))
            slopes[layer, :, columns] = slope
            xs[layer + 1, :, columns] = (xf[:, columns] + value).astype(jnp.bfloat16)
        return carry

    lax.fori_loop(0, LAYERS, ahead, 0)


def run_back(w_buf, xs, slopes, scales, grads, dh_own, beside):
    section = lax.axis_index("section")

    def back(step, carry):
        beside(step)
        layer = LAYERS - 1 - step
        grad = grads[...].astype(jnp.float32)
        d_h = (grad * slopes[layer]).astype(jnp.bfloat16)

        @pl.when(layer == section)
        def _():
            dh_own[...] = d_h

        d_u = None
        for half in range(2):
            w_half = w_buf[half, layer // 2, layer % 2].reshape(WIDTH, HALF)
            term = dot(d_h[:, half * HALF:half * HALF + HALF], w_half, (1, 1))
            d_u = term if d_u is None else d_u + term
        xf = xs[layer].astype(jnp.float32)
        scale = scales[layer, :, 0:1]
        shift = scale * scale * scale * jnp.mean(d_u * xf, axis=-1, keepdims=True)
        grads[...] = (grad + (scale * d_u - xf * shift)).astype(jnp.bfloat16)
        return carry

    lax.fori_loop(0, LAYERS - 1, back, 0)

    @pl.when(section == 0)
    def _():
        dh_own[...] = (grads[...].astype(jnp.float32) * slopes[0]).astype(jnp.bfloat16)


def keep(ref, at, value):
    for i in range(value.shape[1] // 128):
        ref[at + i * HALF:at + i * HALF + HALF, :] = value[:, i * 128:i * 128 + 128]


class Stream:
    def __init__(self, index, refs, sems, x_sems, z_sems):
        self.part, self.acc, self.full, self.got_core, self.got_x, self.got_z = refs
        self.sems, self.index = sems, index
        self.half = self.part.shape[0] // 2
        x, y, z_hi, z_lo, core = place()
        self.core = core
        self.sibling = device(x, y, z_hi, z_lo, 1 - core)
        x_peers = [device((x + k) % 4, y, z_hi, z_lo, core) for k in range(4)]
        z_peers = [device(x, y, z_hi, (z_lo + k) % 8, core) for k in range(8)]
        third = x * (self.half // 4)
        self.ways = {"x": (4, x, 0, x_peers, x_sems, self.got_x), "z": (8, z_lo, third, z_peers, z_sems, self.got_z)}

    def span(self, at, size):
        return pl.ds(pl.multiple_of(at, 8), size)

    def core_copy(self, t):
        half = self.half
        if t == 0:
            src, dst = self.part.at[self.span((1 - self.core) * half, half)], self.got_core
        else:
            src = self.full.at[self.span(self.core * half, half)]
            dst = src
        return pltpu.make_async_remote_copy(
            src_ref=src, dst_ref=dst, send_sem=self.sems.at[0, self.index, t // 5],
            recv_sem=self.sems.at[1, self.index, t // 5], device_id=self.sibling, device_id_type=MESH,
        )

    def copies(self, t, arriving=False):
        count, mine, base, peers, sems, got = self.ways["x" if t in (1, 4) else "z"]
        size = got.shape[1]
        way = 0 if t <= 2 else 1
        made = []
        for k in range(1, count):
            if way == 0:
                src, dst = self.acc.at[self.span(base + (mine + k) % count * size, size)], got.at[k - 1]
            else:
                owner = (mine + count - k) % count if arriving else mine
                src = self.full.at[self.span(self.core * self.half + base + owner * size, size)]
                dst = src
            made.append(pltpu.make_async_remote_copy(
                src_ref=src, dst_ref=dst, send_sem=sems.at[0, way, self.index, k],
                recv_sem=sems.at[1, way, self.index, k], device_id=peers[k], device_id_type=MESH,
            ))
        return made

    def advance(self, t):
        if t > 0:
            done = t - 1
            if done in (0, 5):
                self.core_copy(done).wait_recv()
            else:
                for copy in self.copies(done, True):
                    copy.wait_recv()
            if done == 0:
                self.acc[...] = self.part[self.span(self.core * self.half, self.half), :] + self.got_core[...]
            elif done <= 2:
                count, mine, base, _, _, got = self.ways["x" if done == 1 else "z"]
                size = got.shape[1]
                here = self.span(base + mine * size, size)
                total = self.acc[here, :]
                for k in range(count - 1):
                    total = total + got[k]
                if done == 1:
                    self.acc[here, :] = total
                else:
                    self.full[self.span(self.core * self.half + base + mine * size, size), :] = total
        if t in (0, 5):
            self.core_copy(t).start()
        elif t < 5:
            for copy in self.copies(t):
                copy.start()

    def close(self):
        for t in range(6):
            if t in (0, 5):
                self.core_copy(t).wait_send()
            else:
                for copy in self.copies(t):
                    copy.wait_send()


def load_factor(mats, which, small, large):
    row = lax.broadcasted_iota(jnp.int32, (128, 128), 0)
    lane = lax.broadcasted_iota(jnp.int32, (128, 128), 1)
    shift = jnp.where(row == lane, 0.1, 0.0)
    share = 1.0 / 32768.0

    def put(i, j, value):
        value = value * share
        mats[which, i * 128:i * 128 + 128, j * 128:j * 128 + 128] = value + shift if i == j else value

    for i in range(2):
        for j in range(2):
            low = large[j * HALF + i * 128:j * HALF + i * 128 + 128, :]
            put(i, j, small[j * HALF + i * 128:j * HALF + i * 128 + 128, :])
            put(2 + i, j, low)
            put(j, 2 + i, low.T)
            put(2 + i, 2 + j, large[WIDTH + j * HALF + i * 128:WIDTH + j * HALF + i * 128 + 128, :])


def invert(mats, beside):
    wide_lane = lax.broadcasted_iota(jnp.int32, (64, WIDTH), 1)
    wide_row = lax.broadcasted_iota(jnp.int32, (64, WIDTH), 0)

    def eliminate(block, carry):
        for odd in range(2):
            for b in range(4):
                pl.when(block == b)(functools.partial(beside, 2 * b + odd))
            at = pl.multiple_of(block * 128 + odd * 64, 64)
            rows = pl.ds(at, 64)
            pair = []
            for which in range(2):
                square = mats[which, rows, pl.ds(pl.multiple_of(block * 128, 128), 128)]
                pair.append(square[:, odd * 64:odd * 64 + 64])
            both = jnp.concatenate(pair, axis=1)
            done = jnp.concatenate(sweep_pair([both[8 * i:8 * i + 8] for i in range(8)]), axis=0)
            in_block = (wide_lane >= at) & (wide_lane < at + 64)
            for which in range(2):
                panel = mats[which, rows, :]
                top = jnp.where(in_block, jnp.where(wide_lane - at == wide_row, 1.0, 0.0), -panel)
                fresh = product(done[:, which * 64:which * 64 + 64], top, (1, 0), (1, 0))
                for part in range(2):
                    half = pl.ds(part * 256, 256)
                    step = product(panel[:, part * 256:part * 256 + 256], fresh, (0, 0), (0, 0))
                    mats[which, half, :] = jnp.where(in_block[:1], 0.0, mats[which, half, :]) - step
                mats[which, rows, :] = fresh
        return carry

    lax.fori_loop(0, 4, eliminate, 0)


def packed(ref):
    return jnp.concatenate([ref[i * HALF:i * HALF + HALF, :] for i in range(4)], axis=1)


def kernel(act_ref, cot_ref, w_ref, out_ref, w_buf, xs, slopes, scales, grads, u_own, dh_own, mats, p_mat, *rest):
    gather_refs, sems, x_sems, z_sems, stream_refs = rest[:9], rest[9], rest[10], rest[11], rest[12:]
    rank = lax.axis_index("dp")
    streams = []
    for i in range(6):
        streams.append(Stream(i, stream_refs[6 * i:6 * i + 6], sems, x_sems, z_sems))
    a_small, a_large, g_small, g_large, d_top, d_low = streams

    xs[0] = act_ref[...]
    grads[...] = cot_ref[...]
    gather_weights(w_ref, w_buf, *gather_refs)
    run_ahead(w_buf, xs, slopes, scales, u_own)

    def factor(ref, small, large):
        keep(small.part, 0, dot(ref[:, :HALF], ref[:, :HALF], (0, 0)))
        keep(large.part, 0, dot(ref[:, HALF:], ref[:, :HALF], (0, 0)))
        keep(large.part, WIDTH, dot(ref[:, HALF:], ref[:, HALF:], (0, 0)))

    def advance(group, t):
        for stream in group:
            stream.advance(t)

    in_pair, out_pair, d_pair = streams[:2], streams[2:4], streams[4:]
    factor(u_own, a_small, a_large)
    advance(in_pair, 0)

    def beside_back(step):
        for t, at in ((1, 2), (2, 5)):
            pl.when(step == at)(functools.partial(advance, in_pair, t))

    run_back(w_buf, xs, slopes, scales, grads, dh_own, beside_back)
    factor(dh_own, g_small, g_large)
    advance(out_pair, 0)
    keep(d_top.part, 0, dot(u_own[:, :HALF], dh_own[...], (0, 0)))
    keep(d_low.part, 0, dot(u_own[:, HALF:], dh_own[...], (0, 0)))
    for t in range(1, 7):
        advance(out_pair, t)
        if t + 2 <= 6:
            advance(in_pair, t + 2)
        if t + 2 == 6:
            load_factor(mats, 0, a_small.full, a_large.full)
        if t >= 2:
            advance(d_pair, t - 2)
    load_factor(mats, 1, g_small.full, g_large.full)

    def beside_invert(step):
        if step in (2, 4):
            advance(d_pair, 4 + step // 2)

    invert(mats, beside_invert)
    d_mat = jnp.concatenate([packed(d_top.full), packed(d_low.full)], axis=0)
    p_mat[...] = product_of_halves(mats[0], d_mat)
    p_mat[...] = product_of_halves(p_mat[...], mats[1])
    whole = p_mat[...]
    mean = jnp.sum(jnp.sum(whole * whole, axis=0, keepdims=True), axis=1, keepdims=True) * (1.0 / (WIDTH * WIDTH))
    mine = p_mat[pl.ds(pl.multiple_of(rank * 8, 8), 8), :]
    out_ref[...] = mine / jnp.sqrt(mean + 1e-06)
    for stream in streams:
        stream.close()


def local(first_acts, cotangent, weights):
    square = lambda n, kind: pltpu.VMEM((n, TOKENS, WIDTH), kind)
    flat = lambda kind: pltpu.VMEM((TOKENS, WIDTH), kind)
    copies = pltpu.SemaphoreType.DMA
    scratch = [
        pltpu.VMEM((2, 4, 2, 4, 128, HALF), jnp.bfloat16),
        square(LAYERS + 1, jnp.bfloat16),
        square(LAYERS, jnp.float32),
        pltpu.VMEM((LAYERS, TOKENS, 128), jnp.float32),
        flat(jnp.bfloat16), flat(jnp.bfloat16), flat(jnp.bfloat16),
        square(2, jnp.float32), flat(jnp.float32),
        pltpu.VMEM((8, HALF), jnp.float32),
        pltpu.VMEM((8, HALF), jnp.float32),
        copies((2,)), copies((16,)), copies((16,)),
        copies((4, 16)), copies((4, 16)), copies((4, 16)), copies((4, 16)),
        copies((2, 6, 2)), copies((2, 2, 6, 4)), copies((2, 2, 6, 8)),
    ]
    for rows in (512, 1024, 512, 1024, 1024, 1024):
        sizes = [rows, rows // 2, rows, rows // 2]
        scratch += [pltpu.VMEM((size, 128), jnp.float32) for size in sizes]
        scratch += [pltpu.VMEM((n - 1, rows // (2 * part), 128), jnp.float32) for n, part in ((4, 4), (8, 32))]
    return pl.pallas_call(
        kernel,
        out_shape=jax.ShapeDtypeStruct((8, WIDTH), jnp.float32),
        in_specs=[pl.BlockSpec(memory_space=pltpu.VMEM)] * 3,
        out_specs=pl.BlockSpec(memory_space=pltpu.VMEM),
        scratch_shapes=scratch,
        compiler_params=pltpu.CompilerParams(
            collective_id=0, has_side_effects=True, vmem_limit_bytes=VMEM_LIMIT
        ),
        name="chain_and_factors",
    )(first_acts.reshape(TOKENS, WIDTH), cotangent.reshape(TOKENS, WIDTH), weights)


def solution(mesh):
    placed = (P(None, "dp", None), P(None, "dp", None), P(("section", "dp"), None))
    return jax.shard_map(
        local, mesh=mesh, in_specs=placed, out_specs=P(("section", "dp"), None), check_vma=False
    )
```

```python
import functools

import jax
import jax.numpy as jnp
from jax import lax
from jax.experimental import pallas as pl
from jax.experimental.pallas import tpu as pltpu
from jax.sharding import PartitionSpec as P

MESH = pl.DeviceIdType.MESH
WIDTH = 512
TOKENS = 512
LAYERS = 8
HALF = 256
VMEM_LIMIT = 56 * 1024 * 1024


def place():
    section = lax.axis_index("section")
    rank = lax.axis_index("dp")
    y, z_hi = section // 2, section % 2
    x, z_lo, core = rank // 16, (rank % 16) // 2, rank % 2
    return x, y, z_hi, z_lo, core


def device(x, y, z_hi, z_lo, core):
    return (y * 2 + z_hi, x * 16 + z_lo * 2 + core)


def flip_low(v):
    return v + 1 - 2 * (v % 2)


def send(src, dst, send_sem, recv_sem, target):
    copy = pltpu.make_async_remote_copy(
        src_ref=src, dst_ref=dst, send_sem=send_sem, recv_sem=recv_sem,
        device_id=target, device_id_type=MESH,
    )
    copy.start()
    return copy


def meet(targets):
    barrier = pltpu.get_barrier_semaphore()
    for target in targets:
        pl.semaphore_signal(barrier, inc=1, device_id=target, device_id_type=MESH)
    pl.semaphore_wait(barrier, len(targets))


def gather_weights(w_ref, buf, mine_ref, sib_ref, sib_sem, z_send, z_recv, h_send, h_recv, c_send, c_recv):
    x, y, z_hi, z_lo, core = place()
    z = z_hi * 8 + z_lo
    sibling = device(x, y, z_hi, z_lo, 1 - core)
    z_peers = []
    for k in range(1, 16):
        other = (z + k) % 16
        z_peers.append(device(x, y, other // 8, other % 8, core))
    moves = [
        (lambda a, b: (flip_low(a), b)),
        (lambda a, b: (3 - a, b)),
        (lambda a, b: (a, flip_low(b))),
        (lambda a, b: (a, 3 - b)),
    ]
    orders = [(0, 1, 2, 3), (1, 2, 3, 0), (2, 3, 0, 1), (3, 0, 1, 2)]
    partners = []
    for move in moves:
        px, py = move(x, y)
        partners.append(device(px, py, z_hi, z_lo, core))
    meet([sibling] + z_peers + partners + [device((x + 2) % 4, y, z_hi, z_lo, core)])

    first = core == 0
    wf = w_ref[...].astype(jnp.float32)
    left, right = wf[:, :256], wf[:, 256:]
    mine_ref[...] = jnp.where(first, right, left)
    swap = send(mine_ref, sib_ref, sib_sem.at[0], sib_sem.at[1], sibling)
    mine = jnp.where(first, left, right)
    swap.wait()
    theirs = sib_ref[...]
    rows = jnp.concatenate([jnp.where(first, mine, theirs), jnp.where(first, theirs, mine)], axis=0)
    own = buf.at[core, y, z_hi, x, pl.ds(pl.multiple_of(z_lo * 16, 16), 16), :]
    own[...] = rows.astype(jnp.bfloat16)
    z_copies = [send(own, own, z_send.at[k], z_recv.at[k], z_peers[k - 1]) for k in range(1, 16)]
    for copy in z_copies:
        copy.wait_recv()

    def block(j, at):
        bx, by = at
        return buf.at[core, by, j // 2, bx, pl.ds((j % 2) * 64, 64), :]

    held = {}
    copies = {}
    across = {}

    def forward(j, r, step_from):
        ref = block(j, held[j, r])
        for step in range(step_from, 4):
            index = 2 ** step + r
            copies[j, index] = send(
                ref, ref, h_send.at[j, index], h_recv.at[j, index], partners[orders[j][step]]
            )
        across[j, r] = send(ref, ref, c_send.at[j, r], c_recv.at[j, r], sibling)

    for j in range(4):
        held[j, 0] = (x, y)
        for r in range(1, 16):
            step = r.bit_length() - 1
            held[j, r] = moves[orders[j][step]](*held[j, r - 2 ** step])
    for j in range(4):
        forward(j, 0, 0)
    arrivals = sorted(range(1, 16), key=lambda r: (bin(r).count("1"), r))
    for r in arrivals:
        for j in range(4):
            copies[j, r].wait_recv()
            forward(j, r, r.bit_length())
    for j in range(4):
        for r in range(16):
            across[j, r].wait_recv()
    for copy in z_copies:
        copy.wait_send()
    for j in range(4):
        for r in range(16):
            across[j, r].wait_send()
            if r:
                copies[j, r].wait_send()


def gelu_parts(h):
    coeff = 0.7978845608028654
    inner = coeff * (h + 0.044715 * h * h * h)
    tanh_val = jnp.tanh(inner)
    value = 0.5 * h * (1.0 + tanh_val)
    slope = 0.5 * (1.0 + tanh_val) + 0.5 * h * (1.0 - tanh_val * tanh_val) * coeff * (
        1.0 + 3.0 * 0.044715 * h * h
    )
    return (value, slope)


def dot(a, b, dims):
    return lax.dot_general(
        a, b, ((dims[:1], dims[1:]), ((), ())), preferred_element_type=jnp.float32
    )


def splat(value):
    return jnp.broadcast_to(value, (8, 128))


def thirds(value):
    high = value.astype(jnp.bfloat16).astype(jnp.float32)
    rest = value - high
    middle = rest.astype(jnp.bfloat16).astype(jnp.float32)
    return high, middle, rest - middle


def product(a, b, dims, axes):
    a0, a1, a2 = thirds(a)
    b0, b1, b2 = thirds(b)
    long_a = jnp.concatenate([a0, a0, a1, a1, a0, a2], axis=axes[0]).astype(jnp.bfloat16)
    long_b = jnp.concatenate([b0, b1, b0, b1, b2, b0], axis=axes[1]).astype(jnp.bfloat16)
    return dot(long_a, long_b, dims)


def halves(value):
    high = value.astype(jnp.bfloat16)
    return high, (value - high.astype(jnp.float32)).astype(jnp.bfloat16)


def product_of_halves(a, b):
    a0, a1 = halves(a)
    b0, b1 = halves(b)
    return dot(a0, b0, (1, 0)) + (dot(a0, b1, (1, 0)) + dot(a1, b0, (1, 0)))


def minus_inverse(e):
    at = lambda i, k: (min(i, k), max(i, k))
    for k in range(0, 8, 2):
        a, b, c = e[k, k], e[k, k + 1], e[k + 1, k + 1]
        scale = 1.0 / (a * c - b * b)
        ia, ib, ic = c * scale, -(b * scale), a * scale
        others = [i for i in range(8) if i not in (k, k + 1)]
        r0 = {i: ia * e[at(i, k)] + ib * e[at(i, k + 1)] for i in others}
        r1 = {i: ib * e[at(i, k)] + ic * e[at(i, k + 1)] for i in others}
        for i in others:
            for j in others:
                if i <= j:
                    e[i, j] = e[i, j] - (e[at(i, k)] * r0[j] + e[at(i, k + 1)] * r1[j])
        for i in others:
            e[at(i, k)], e[at(i, k + 1)] = r0[i], r1[i]
        e[k, k], e[k, k + 1], e[k + 1, k + 1] = -ia, -ib, -ic
    return lambda i, k: e[at(i, k)]


def sweep_pair(tiles):
    tiles = list(tiles)
    lane = lax.broadcasted_iota(jnp.int32, (8, 128), 1)
    row = lax.broadcasted_iota(jnp.int32, (8, 128), 0)
    first = lane < 64
    local_lane = lane % 64

    def column(tile, k):
        return jnp.where(first, splat(tile[:, k:k + 1]), splat(tile[:, 64 + k:65 + k]))

    for p in range(8):
        pivot = tiles[p]
        base = 8 * p
        in_block = (local_lane >= base) & (local_lane < base + 8)
        columns = [column(pivot, base + k) for k in range(8)]
        e = {}
        for k in range(8):
            for i in range(k + 1):
                e[i, k] = splat(columns[k][i:i + 1, :])
        inverse = minus_inverse(e)
        top = jnp.where(in_block, jnp.where(local_lane - base == row, 1.0, 0.0), -pivot)
        result = None
        for k in range(8):
            spread = inverse(0, k)
            for i in range(1, 8):
                spread = jnp.where(row == i, inverse(i, k), spread)
            term = spread * splat(top[k:k + 1, :])
            result = term if result is None else result + term
        tiles[p] = result
        if p < 7:
            value = jnp.where(in_block, 0.0, tiles[p + 1])
            for k in range(8):
                value = value - column(tiles[p + 1], base + k) * splat(result[k:k + 1, :])
        update = product(pivot, result, (0, 0), (0, 0))
        for i in range(8):
            if i not in (p, p + 1):
                step = jnp.where(first, update[8 * i:8 * i + 8], update[64 + 8 * i:72 + 8 * i])
                tiles[i] = jnp.where(in_block, 0.0, tiles[i]) - step
        if p < 7:
            tiles[p + 1] = value
    return tiles


def run_ahead(w_buf, xs, slopes, scales, units):
    def ahead(layer, carry):
        xf = xs[layer].astype(jnp.float32)
        scale = lax.rsqrt(jnp.mean(xf * xf, axis=-1, keepdims=True) + 1e-05)
        scales[layer] = jnp.broadcast_to(scale, (TOKENS, 128))
        unit = (xf * scale).astype(jnp.bfloat16)

        units[layer] = unit
        for half in range(2):
            columns = slice(half * HALF, half * HALF + HALF)
            w_half = w_buf[half, layer // 2, layer % 2].reshape(WIDTH, HALF)
            value, slope = gelu_parts(dot(unit, w_half, (1, 0)))
            slopes[layer, :, columns] = slope
            xs[layer + 1, :, columns] = (xf[:, columns] + value).astype(jnp.bfloat16)
        return carry

    lax.fori_loop(0, LAYERS, ahead, 0)


def run_back(w_buf, xs, slopes, scales, grads, slants, beside):
    def back(step, carry):
        beside(step)
        layer = LAYERS - 1 - step
        grad = grads[...].astype(jnp.float32)
        d_h = (grad * slopes[layer]).astype(jnp.bfloat16)

        slants[layer] = d_h
        d_u = None
        for half in range(2):
            w_half = w_buf[half, layer // 2, layer % 2].reshape(WIDTH, HALF)
            term = dot(d_h[:, half * HALF:half * HALF + HALF], w_half, (1, 1))
            d_u = term if d_u is None else d_u + term
        xf = xs[layer].astype(jnp.float32)
        scale = scales[layer, :, 0:1]
        shift = scale * scale * scale * jnp.mean(d_u * xf, axis=-1, keepdims=True)
        grads[...] = (grad + (scale * d_u - xf * shift)).astype(jnp.bfloat16)
        return carry

    lax.fori_loop(0, LAYERS - 1, back, 0)
    slants[0] = (grads[...].astype(jnp.float32) * slopes[0]).astype(jnp.bfloat16)


def keep(ref, at, value):
    for i in range(value.shape[1] // 128):
        ref[at + i * HALF:at + i * HALF + HALF, :] = value[:, i * 128:i * 128 + 128]


class Stream:
    def __init__(self, index, refs, sems, x_sems, z_sems):
        self.part, self.acc, self.full, self.got_core, self.got_x, self.got_z = refs
        self.sems, self.index = sems, index
        self.half = self.part.shape[0] // 2
        x, y, z_hi, z_lo, core = place()
        self.core = core
        self.sibling = device(x, y, z_hi, z_lo, 1 - core)
        x_peers = [device((x + k) % 4, y, z_hi, z_lo, core) for k in range(4)]
        z_peers = [device(x, y, z_hi, (z_lo + k) % 8, core) for k in range(8)]
        third = x * (self.half // 4)
        self.ways = {"x": (4, x, 0, x_peers, x_sems, self.got_x), "z": (8, z_lo, third, z_peers, z_sems, self.got_z)}

    def span(self, at, size):
        return pl.ds(pl.multiple_of(at, 8), size)

    def core_copy(self, t):
        half = self.half
        if t == 0:
            src, dst = self.part.at[self.span((1 - self.core) * half, half)], self.got_core
        else:
            src = self.full.at[self.span(self.core * half, half)]
            dst = src
        return pltpu.make_async_remote_copy(
            src_ref=src, dst_ref=dst, send_sem=self.sems.at[0, self.index, t // 5],
            recv_sem=self.sems.at[1, self.index, t // 5], device_id=self.sibling, device_id_type=MESH,
        )

    def copies(self, t, arriving=False):
        count, mine, base, peers, sems, got = self.ways["x" if t in (1, 4) else "z"]
        size = got.shape[1]
        way = 0 if t <= 2 else 1
        made = []
        for k in range(1, count):
            if way == 0:
                src, dst = self.acc.at[self.span(base + (mine + k) % count * size, size)], got.at[k - 1]
            else:
                owner = (mine + count - k) % count if arriving else mine
                src = self.full.at[self.span(self.core * self.half + base + owner * size, size)]
                dst = src
            made.append(pltpu.make_async_remote_copy(
                src_ref=src, dst_ref=dst, send_sem=sems.at[0, way, self.index, k],
                recv_sem=sems.at[1, way, self.index, k], device_id=peers[k], device_id_type=MESH,
            ))
        return made

    def advance(self, t):
        if t > 0:
            done = t - 1
            if done in (0, 5):
                self.core_copy(done).wait_recv()
            else:
                for copy in self.copies(done, True):
                    copy.wait_recv()
            if done == 0:
                self.acc[...] = self.part[self.span(self.core * self.half, self.half), :] + self.got_core[...]
            elif done <= 2:
                count, mine, base, _, _, got = self.ways["x" if done == 1 else "z"]
                size = got.shape[1]
                here = self.span(base + mine * size, size)
                total = self.acc[here, :]
                for k in range(count - 1):
                    total = total + got[k]
                if done == 1:
                    self.acc[here, :] = total
                else:
                    self.full[self.span(self.core * self.half + base + mine * size, size), :] = total
        if t in (0, 5):
            self.core_copy(t).start()
        elif t < 5:
            for copy in self.copies(t):
                copy.start()

    def close(self):
        for t in range(6):
            if t in (0, 5):
                self.core_copy(t).wait_send()
            else:
                for copy in self.copies(t):
                    copy.wait_send()


def load_factor(mats, which, small, large):
    row = lax.broadcasted_iota(jnp.int32, (128, 128), 0)
    lane = lax.broadcasted_iota(jnp.int32, (128, 128), 1)
    shift = jnp.where(row == lane, 0.1, 0.0)
    share = 1.0 / 32768.0

    def put(i, j, value):
        value = value * share
        mats[which, i * 128:i * 128 + 128, j * 128:j * 128 + 128] = value + shift if i == j else value

    for i in range(2):
        for j in range(2):
            low = large[j * HALF + i * 128:j * HALF + i * 128 + 128, :]
            put(i, j, small[j * HALF + i * 128:j * HALF + i * 128 + 128, :])
            put(2 + i, j, low)
            put(j, 2 + i, low.T)
            put(2 + i, 2 + j, large[WIDTH + j * HALF + i * 128:WIDTH + j * HALF + i * 128 + 128, :])


def invert(mats, beside):
    wide_lane = lax.broadcasted_iota(jnp.int32, (64, WIDTH), 1)
    wide_row = lax.broadcasted_iota(jnp.int32, (64, WIDTH), 0)

    def eliminate(block, carry):
        for odd in range(2):
            for b in range(4):
                pl.when(block == b)(functools.partial(beside, 2 * b + odd))
            at = pl.multiple_of(block * 128 + odd * 64, 64)
            rows = pl.ds(at, 64)
            pair = []
            for which in range(2):
                square = mats[which, rows, pl.ds(pl.multiple_of(block * 128, 128), 128)]
                pair.append(square[:, odd * 64:odd * 64 + 64])
            both = jnp.concatenate(pair, axis=1)
            done = jnp.concatenate(sweep_pair([both[8 * i:8 * i + 8] for i in range(8)]), axis=0)
            in_block = (wide_lane >= at) & (wide_lane < at + 64)
            for which in range(2):
                panel = mats[which, rows, :]
                top = jnp.where(in_block, jnp.where(wide_lane - at == wide_row, 1.0, 0.0), -panel)
                fresh = product(done[:, which * 64:which * 64 + 64], top, (1, 0), (1, 0))
                if which == 0:
                    p0, p1 = halves(panel)
                    f0, f1 = halves(fresh)
                    wide, long = [p0, p0, p1], [f0, f1, f0]
                else:
                    p0, p1, p2 = thirds(panel)
                    f0, f1, f2 = thirds(fresh)
                    wide, long = [p0, p0, p1, p1, p0, p2], [f0, f1, f0, f1, f2, f0]
                wide = jnp.concatenate(wide, axis=0).astype(jnp.bfloat16)
                long = jnp.concatenate(long, axis=0).astype(jnp.bfloat16)
                for part in range(2):
                    half = pl.ds(part * 256, 256)
                    step = dot(wide[:, part * 256:part * 256 + 256], long, (0, 0))
                    mats[which, half, :] = jnp.where(in_block[:1], 0.0, mats[which, half, :]) - step
                mats[which, rows, :] = fresh
        return carry

    lax.fori_loop(0, 4, eliminate, 0)


def packed(ref):
    return jnp.concatenate([ref[i * HALF:i * HALF + HALF, :] for i in range(4)], axis=1)


def kernel(act_ref, cot_ref, w_ref, out_ref, w_buf, xs, slopes, scales, grads, units, slants, mats, p_mat, *rest):
    gather_refs, sems, x_sems, z_sems, stream_refs = rest[:9], rest[9], rest[10], rest[11], rest[12:]
    section, rank = lax.axis_index("section"), lax.axis_index("dp")
    streams = []
    for i in range(6):
        streams.append(Stream(i, stream_refs[6 * i:6 * i + 6], sems, x_sems, z_sems))
    a_small, a_large, g_small, g_large, d_top, d_low = streams

    xs[0] = act_ref[...]
    grads[...] = cot_ref[...]
    gather_weights(w_ref, w_buf, *gather_refs)
    run_ahead(w_buf, xs, slopes, scales, units)
    u_own, dh_own = units.at[section], slants.at[section]

    def factor(ref, small, large):
        keep(small.part, 0, dot(ref[:, :HALF], ref[:, :HALF], (0, 0)))
        keep(large.part, 0, dot(ref[:, HALF:], ref[:, :HALF], (0, 0)))
        keep(large.part, WIDTH, dot(ref[:, HALF:], ref[:, HALF:], (0, 0)))

    def advance(group, t):
        for stream in group:
            stream.advance(t)

    in_pair, out_pair, d_pair = streams[:2], streams[2:4], streams[4:]
    factor(u_own, a_small, a_large)
    advance(in_pair, 0)

    def beside_back(step):
        for t, at in ((1, 2), (2, 5)):
            pl.when(step == at)(functools.partial(advance, in_pair, t))

    run_back(w_buf, xs, slopes, scales, grads, slants, beside_back)
    factor(dh_own, g_small, g_large)
    advance(out_pair, 0)
    keep(d_top.part, 0, dot(u_own[:, :HALF], dh_own[...], (0, 0)))
    keep(d_low.part, 0, dot(u_own[:, HALF:], dh_own[...], (0, 0)))
    for t in range(1, 7):
        advance(out_pair, t)
        if t + 2 <= 6:
            advance(in_pair, t + 2)
        if t + 2 == 6:
            load_factor(mats, 0, a_small.full, a_large.full)
        if t >= 2:
            advance(d_pair, t - 2)
    load_factor(mats, 1, g_small.full, g_large.full)

    def beside_invert(step):
        if step in (2, 4):
            advance(d_pair, 4 + step // 2)

    invert(mats, beside_invert)
    d_mat = jnp.concatenate([packed(d_top.full), packed(d_low.full)], axis=0)
    p_mat[...] = product_of_halves(mats[0], d_mat)
    p_mat[...] = product_of_halves(p_mat[...], mats[1])
    whole = p_mat[...]
    mean = jnp.sum(jnp.sum(whole * whole, axis=0, keepdims=True), axis=1, keepdims=True) * (1.0 / (WIDTH * WIDTH))
    mine = p_mat[pl.ds(pl.multiple_of(rank * 8, 8), 8), :]
    out_ref[...] = mine / jnp.sqrt(mean + 1e-06)
    for stream in streams:
        stream.close()


def local(first_acts, cotangent, weights):
    square = lambda n, kind: pltpu.VMEM((n, TOKENS, WIDTH), kind)
    flat = lambda kind: pltpu.VMEM((TOKENS, WIDTH), kind)
    copies = pltpu.SemaphoreType.DMA
    scratch = [
        pltpu.VMEM((2, 4, 2, 4, 128, HALF), jnp.bfloat16),
        square(LAYERS + 1, jnp.bfloat16),
        square(LAYERS, jnp.float32),
        pltpu.VMEM((LAYERS, TOKENS, 128), jnp.float32),
        flat(jnp.bfloat16), square(LAYERS, jnp.bfloat16), square(LAYERS, jnp.bfloat16),
        square(2, jnp.float32), flat(jnp.float32),
        pltpu.VMEM((8, HALF), jnp.float32),
        pltpu.VMEM((8, HALF), jnp.float32),
        copies((2,)), copies((16,)), copies((16,)),
        copies((4, 16)), copies((4, 16)), copies((4, 16)), copies((4, 16)),
        copies((2, 6, 2)), copies((2, 2, 6, 4)), copies((2, 2, 6, 8)),
    ]
    for rows in (512, 1024, 512, 1024, 1024, 1024):
        sizes = [rows, rows // 2, rows, rows // 2]
        scratch += [pltpu.VMEM((size, 128), jnp.float32) for size in sizes]
        scratch += [pltpu.VMEM((n - 1, rows // (2 * part), 128), jnp.float32) for n, part in ((4, 4), (8, 32))]
    return pl.pallas_call(
        kernel,
        out_shape=jax.ShapeDtypeStruct((8, WIDTH), jnp.float32),
        in_specs=[pl.BlockSpec(memory_space=pltpu.VMEM)] * 3,
        out_specs=pl.BlockSpec(memory_space=pltpu.VMEM),
        scratch_shapes=scratch,
        compiler_params=pltpu.CompilerParams(
            collective_id=0, has_side_effects=True, vmem_limit_bytes=VMEM_LIMIT
        ),
        name="chain_and_factors",
    )(first_acts.reshape(TOKENS, WIDTH), cotangent.reshape(TOKENS, WIDTH), weights)


def solution(mesh):
    placed = (P(None, "dp", None), P(None, "dp", None), P(("section", "dp"), None))
    return jax.shard_map(
        local, mesh=mesh, in_specs=placed, out_specs=P(("section", "dp"), None), check_vma=False
    )
```

```python
import functools

import jax
import jax.numpy as jnp
from jax import lax
from jax.experimental import pallas as pl
from jax.experimental.pallas import tpu as pltpu
from jax.sharding import PartitionSpec as P

MESH = pl.DeviceIdType.MESH
WIDTH = 512
TOKENS = 512
LAYERS = 8
HALF = 256
VMEM_LIMIT = 56 * 1024 * 1024


def place():
    section = lax.axis_index("section")
    rank = lax.axis_index("dp")
    y, z_hi = section // 2, section % 2
    x, z_lo, core = rank // 16, (rank % 16) // 2, rank % 2
    return x, y, z_hi, z_lo, core


def device(x, y, z_hi, z_lo, core):
    return (y * 2 + z_hi, x * 16 + z_lo * 2 + core)


def flip_low(v):
    return v + 1 - 2 * (v % 2)


def send(src, dst, send_sem, recv_sem, target):
    copy = pltpu.make_async_remote_copy(
        src_ref=src, dst_ref=dst, send_sem=send_sem, recv_sem=recv_sem,
        device_id=target, device_id_type=MESH,
    )
    copy.start()
    return copy


def meet(targets):
    barrier = pltpu.get_barrier_semaphore()
    for target in targets:
        pl.semaphore_signal(barrier, inc=1, device_id=target, device_id_type=MESH)
    pl.semaphore_wait(barrier, len(targets))


def gather_weights(w_ref, buf, mine_ref, sib_ref, sib_sem, z_send, z_recv, h_send, h_recv, c_send, c_recv):
    x, y, z_hi, z_lo, core = place()
    z = z_hi * 8 + z_lo
    sibling = device(x, y, z_hi, z_lo, 1 - core)
    z_peers = []
    for k in range(1, 16):
        other = (z + k) % 16
        z_peers.append(device(x, y, other // 8, other % 8, core))
    moves = [
        (lambda a, b: (flip_low(a), b)),
        (lambda a, b: (3 - a, b)),
        (lambda a, b: (a, flip_low(b))),
        (lambda a, b: (a, 3 - b)),
    ]
    orders = [(0, 1, 2, 3), (1, 2, 3, 0), (2, 3, 0, 1), (3, 0, 1, 2)]
    partners = []
    for move in moves:
        px, py = move(x, y)
        partners.append(device(px, py, z_hi, z_lo, core))
    meet([sibling] + z_peers + partners + [device((x + 2) % 4, y, z_hi, z_lo, core)])

    first = core == 0
    wf = w_ref[...].astype(jnp.float32)
    left, right = wf[:, :256], wf[:, 256:]
    mine_ref[...] = jnp.where(first, right, left)
    swap = send(mine_ref, sib_ref, sib_sem.at[0], sib_sem.at[1], sibling)
    mine = jnp.where(first, left, right)
    swap.wait()
    theirs = sib_ref[...]
    rows = jnp.concatenate([jnp.where(first, mine, theirs), jnp.where(first, theirs, mine)], axis=0)
    own = buf.at[core, y, z_hi, x, pl.ds(pl.multiple_of(z_lo * 16, 16), 16), :]
    own[...] = rows.astype(jnp.bfloat16)
    z_copies = [send(own, own, z_send.at[k], z_recv.at[k], z_peers[k - 1]) for k in range(1, 16)]
    for copy in z_copies:
        copy.wait_recv()

    def block(j, at):
        bx, by = at
        return buf.at[core, by, j // 2, bx, pl.ds((j % 2) * 64, 64), :]

    held = {}
    copies = {}
    across = {}

    def forward(j, r, step_from):
        ref = block(j, held[j, r])
        for step in range(step_from, 4):
            index = 2 ** step + r
            copies[j, index] = send(
                ref, ref, h_send.at[j, index], h_recv.at[j, index], partners[orders[j][step]]
            )
        across[j, r] = send(ref, ref, c_send.at[j, r], c_recv.at[j, r], sibling)

    for j in range(4):
        held[j, 0] = (x, y)
        for r in range(1, 16):
            step = r.bit_length() - 1
            held[j, r] = moves[orders[j][step]](*held[j, r - 2 ** step])
    for j in range(4):
        forward(j, 0, 0)
    arrivals = sorted(range(1, 16), key=lambda r: (bin(r).count("1"), r))
    for r in arrivals:
        for j in range(4):
            copies[j, r].wait_recv()
            forward(j, r, r.bit_length())
    for j in range(4):
        for r in range(16):
            across[j, r].wait_recv()
    for copy in z_copies:
        copy.wait_send()
    for j in range(4):
        for r in range(16):
            across[j, r].wait_send()
            if r:
                copies[j, r].wait_send()


def gelu_parts(h):
    coeff = 0.7978845608028654
    inner = coeff * (h + 0.044715 * h * h * h)
    tanh_val = jnp.tanh(inner)
    value = 0.5 * h * (1.0 + tanh_val)
    slope = 0.5 * (1.0 + tanh_val) + 0.5 * h * (1.0 - tanh_val * tanh_val) * coeff * (
        1.0 + 3.0 * 0.044715 * h * h
    )
    return (value, slope)


def dot(a, b, dims):
    return lax.dot_general(
        a, b, ((dims[:1], dims[1:]), ((), ())), preferred_element_type=jnp.float32
    )


def splat(value):
    return jnp.broadcast_to(value, (8, 128))


def thirds(value):
    high = value.astype(jnp.bfloat16).astype(jnp.float32)
    rest = value - high
    middle = rest.astype(jnp.bfloat16).astype(jnp.float32)
    return high, middle, rest - middle


def product(a, b, dims, axes):
    a0, a1, a2 = thirds(a)
    b0, b1, b2 = thirds(b)
    long_a = jnp.concatenate([a0, a0, a1, a1, a0, a2], axis=axes[0]).astype(jnp.bfloat16)
    long_b = jnp.concatenate([b0, b1, b0, b1, b2, b0], axis=axes[1]).astype(jnp.bfloat16)
    return dot(long_a, long_b, dims)


def halves(value):
    high = value.astype(jnp.bfloat16)
    return high, (value - high.astype(jnp.float32)).astype(jnp.bfloat16)


def product_of_halves(a, b):
    a0, a1 = halves(a)
    b0, b1 = halves(b)
    return dot(a0, b0, (1, 0)) + (dot(a0, b1, (1, 0)) + dot(a1, b0, (1, 0)))


def minus_inverse(e):
    at = lambda i, k: (min(i, k), max(i, k))
    for k in range(0, 8, 2):
        a, b, c = e[k, k], e[k, k + 1], e[k + 1, k + 1]
        scale = 1.0 / (a * c - b * b)
        ia, ib, ic = c * scale, -(b * scale), a * scale
        others = [i for i in range(8) if i not in (k, k + 1)]
        r0 = {i: ia * e[at(i, k)] + ib * e[at(i, k + 1)] for i in others}
        r1 = {i: ib * e[at(i, k)] + ic * e[at(i, k + 1)] for i in others}
        for i in others:
            for j in others:
                if i <= j:
                    e[i, j] = e[i, j] - (e[at(i, k)] * r0[j] + e[at(i, k + 1)] * r1[j])
        for i in others:
            e[at(i, k)], e[at(i, k + 1)] = r0[i], r1[i]
        e[k, k], e[k, k + 1], e[k + 1, k + 1] = -ia, -ib, -ic
    return lambda i, k: e[at(i, k)]


def sweep_pair(tiles):
    tiles = list(tiles)
    lane = lax.broadcasted_iota(jnp.int32, (8, 128), 1)
    row = lax.broadcasted_iota(jnp.int32, (8, 128), 0)
    first = lane < 64
    local_lane = lane % 64

    def column(tile, k):
        return jnp.where(first, splat(tile[:, k:k + 1]), splat(tile[:, 64 + k:65 + k]))

    for p in range(8):
        pivot = tiles[p]
        base = 8 * p
        in_block = (local_lane >= base) & (local_lane < base + 8)
        columns = [column(pivot, base + k) for k in range(8)]
        e = {}
        for k in range(8):
            for i in range(k + 1):
                e[i, k] = splat(columns[k][i:i + 1, :])
        inverse = minus_inverse(e)
        top = jnp.where(in_block, jnp.where(local_lane - base == row, 1.0, 0.0), -pivot)
        result = None
        for k in range(8):
            spread = inverse(0, k)
            for i in range(1, 8):
                spread = jnp.where(row == i, inverse(i, k), spread)
            term = spread * splat(top[k:k + 1, :])
            result = term if result is None else result + term
        tiles[p] = result
        if p < 7:
            value = jnp.where(in_block, 0.0, tiles[p + 1])
            for k in range(8):
                value = value - column(tiles[p + 1], base + k) * splat(result[k:k + 1, :])
        update = product(pivot, result, (0, 0), (0, 0))
        for i in range(8):
            if i not in (p, p + 1):
                step = jnp.where(first, update[8 * i:8 * i + 8], update[64 + 8 * i:72 + 8 * i])
                tiles[i] = jnp.where(in_block, 0.0, tiles[i]) - step
        if p < 7:
            tiles[p + 1] = value
    return tiles


def run_ahead(w_buf, xs, slopes, scales, units):
    def ahead(layer, carry):
        xf = xs[layer].astype(jnp.float32)
        scale = lax.rsqrt(jnp.mean(xf * xf, axis=-1, keepdims=True) + 1e-05)
        scales[layer] = jnp.broadcast_to(scale, (TOKENS, 128))
        unit = (xf * scale).astype(jnp.bfloat16)

        units[layer] = unit
        for half in range(2):
            columns = slice(half * HALF, half * HALF + HALF)
            w_half = w_buf[half, layer // 2, layer % 2].reshape(WIDTH, HALF)
            value, slope = gelu_parts(dot(unit, w_half, (1, 0)))
            slopes[layer, :, columns] = slope
            xs[layer + 1, :, columns] = (xf[:, columns] + value).astype(jnp.bfloat16)
        return carry

    lax.fori_loop(0, LAYERS, ahead, 0)


def run_back(w_buf, xs, slopes, scales, grads, slants, beside):
    def back(step, carry):
        beside(step)
        layer = LAYERS - 1 - step
        grad = grads[...].astype(jnp.float32)
        d_h = (grad * slopes[layer]).astype(jnp.bfloat16)

        slants[layer] = d_h
        d_u = None
        for half in range(2):
            w_half = w_buf[half, layer // 2, layer % 2].reshape(WIDTH, HALF)
            term = dot(d_h[:, half * HALF:half * HALF + HALF], w_half, (1, 1))
            d_u = term if d_u is None else d_u + term
        xf = xs[layer].astype(jnp.float32)
        scale = scales[layer, :, 0:1]
        shift = scale * scale * scale * jnp.mean(d_u * xf, axis=-1, keepdims=True)
        grads[...] = (grad + (scale * d_u - xf * shift)).astype(jnp.bfloat16)
        return carry

    lax.fori_loop(0, LAYERS - 1, back, 0)
    slants[0] = (grads[...].astype(jnp.float32) * slopes[0]).astype(jnp.bfloat16)


def keep(ref, at, value):
    for i in range(value.shape[1] // 128):
        ref[at + i * HALF:at + i * HALF + HALF, :] = value[:, i * 128:i * 128 + 128]


class Stream:
    def __init__(self, index, refs, sems, x_sems, z_sems):
        self.part, self.acc, self.full, self.got_core, self.got_x, self.got_z = refs
        self.sems, self.index = sems, index
        self.half = self.part.shape[0] // 2
        x, y, z_hi, z_lo, core = place()
        self.core = core
        self.sibling = device(x, y, z_hi, z_lo, 1 - core)
        x_peers = [device((x + k) % 4, y, z_hi, z_lo, core) for k in range(4)]
        z_peers = [device(x, y, z_hi, (z_lo + k) % 8, core) for k in range(8)]
        third = x * (self.half // 4)
        self.ways = {"x": (4, x, 0, x_peers, x_sems, self.got_x), "z": (8, z_lo, third, z_peers, z_sems, self.got_z)}

    def span(self, at, size):
        return pl.ds(pl.multiple_of(at, 8), size)

    def core_copy(self, t):
        half = self.half
        if t == 0:
            src, dst = self.part.at[self.span((1 - self.core) * half, half)], self.got_core
        else:
            src = self.full.at[self.span(self.core * half, half)]
            dst = src
        return pltpu.make_async_remote_copy(
            src_ref=src, dst_ref=dst, send_sem=self.sems.at[0, self.index, t // 5],
            recv_sem=self.sems.at[1, self.index, t // 5], device_id=self.sibling, device_id_type=MESH,
        )

    def copies(self, t, arriving=False):
        count, mine, base, peers, sems, got = self.ways["x" if t in (1, 4) else "z"]
        size = got.shape[1]
        way = 0 if t <= 2 else 1
        made = []
        for k in range(1, count):
            if way == 0:
                src, dst = self.acc.at[self.span(base + (mine + k) % count * size, size)], got.at[k - 1]
            else:
                owner = (mine + count - k) % count if arriving else mine
                src = self.full.at[self.span(self.core * self.half + base + owner * size, size)]
                dst = src
            made.append(pltpu.make_async_remote_copy(
                src_ref=src, dst_ref=dst, send_sem=sems.at[0, way, self.index, k],
                recv_sem=sems.at[1, way, self.index, k], device_id=peers[k], device_id_type=MESH,
            ))
        return made

    def advance(self, t):
        if t > 0:
            done = t - 1
            if done in (0, 5):
                self.core_copy(done).wait_recv()
            else:
                for copy in self.copies(done, True):
                    copy.wait_recv()
            if done == 0:
                self.acc[...] = self.part[self.span(self.core * self.half, self.half), :] + self.got_core[...]
            elif done <= 2:
                count, mine, base, _, _, got = self.ways["x" if done == 1 else "z"]
                size = got.shape[1]
                here = self.span(base + mine * size, size)
                total = self.acc[here, :]
                for k in range(count - 1):
                    total = total + got[k]
                if done == 1:
                    self.acc[here, :] = total
                else:
                    self.full[self.span(self.core * self.half + base + mine * size, size), :] = total
        if t in (0, 5):
            self.core_copy(t).start()
        elif t < 5:
            for copy in self.copies(t):
                copy.start()

    def close(self):
        for t in range(6):
            if t in (0, 5):
                self.core_copy(t).wait_send()
            else:
                for copy in self.copies(t):
                    copy.wait_send()


def load_factor(mats, which, small, large):
    row = lax.broadcasted_iota(jnp.int32, (128, 128), 0)
    lane = lax.broadcasted_iota(jnp.int32, (128, 128), 1)
    shift = jnp.where(row == lane, 0.1, 0.0)
    share = 1.0 / 32768.0

    def put(i, j, value):
        value = value * share
        mats[which, i * 128:i * 128 + 128, j * 128:j * 128 + 128] = value + shift if i == j else value

    for i in range(2):
        for j in range(2):
            low = large[j * HALF + i * 128:j * HALF + i * 128 + 128, :]
            put(i, j, small[j * HALF + i * 128:j * HALF + i * 128 + 128, :])
            put(2 + i, j, low)
            put(j, 2 + i, low.T)
            put(2 + i, 2 + j, large[WIDTH + j * HALF + i * 128:WIDTH + j * HALF + i * 128 + 128, :])


def invert(mats, beside):
    wide_lane = lax.broadcasted_iota(jnp.int32, (64, WIDTH), 1)
    wide_row = lax.broadcasted_iota(jnp.int32, (64, WIDTH), 0)

    def eliminate(block, carry):
        for odd in range(2):
            for b in range(4):
                pl.when(block == b)(functools.partial(beside, 2 * b + odd))
            at = pl.multiple_of(block * 128 + odd * 64, 64)
            rows = pl.ds(at, 64)
            pair = []
            for which in range(2):
                square = mats[which, rows, pl.ds(pl.multiple_of(block * 128, 128), 128)]
                pair.append(square[:, odd * 64:odd * 64 + 64])
            both = jnp.concatenate(pair, axis=1)
            done = jnp.concatenate(sweep_pair([both[8 * i:8 * i + 8] for i in range(8)]), axis=0)
            in_block = (wide_lane >= at) & (wide_lane < at + 64)
            for which in range(2):
                panel = mats[which, rows, :]
                top = jnp.where(in_block, jnp.where(wide_lane - at == wide_row, 1.0, 0.0), -panel)
                fresh = product(done[:, which * 64:which * 64 + 64], top, (1, 0), (1, 0))
                if which == 0:
                    p0, p1 = halves(panel)
                    f0, f1 = halves(fresh)
                    wide, long = [p0, p0, p1], [f0, f1, f0]
                else:
                    p0, p1, p2 = thirds(panel)
                    f0, f1, f2 = thirds(fresh)
                    wide, long = [p0, p0, p1, p1, p0, p2], [f0, f1, f0, f1, f2, f0]
                wide = jnp.concatenate(wide, axis=0).astype(jnp.bfloat16)
                long = jnp.concatenate(long, axis=0).astype(jnp.bfloat16)
                for part in range(2):
                    half = pl.ds(part * 256, 256)
                    step = dot(wide[:, part * 256:part * 256 + 256], long, (0, 0))
                    mats[which, half, :] = jnp.where(in_block[:1], 0.0, mats[which, half, :]) - step
                mats[which, rows, :] = fresh
        return carry

    lax.fori_loop(0, 4, eliminate, 0)


def packed(ref):
    return jnp.concatenate([ref[i * HALF:i * HALF + HALF, :] for i in range(4)], axis=1)


def kernel(act_ref, cot_ref, w_ref, out_ref, w_buf, xs, slopes, scales, grads, units, slants, mats, p_mat, *rest):
    gather_refs, sems, x_sems, z_sems, stream_refs = rest[:9], rest[9], rest[10], rest[11], rest[12:]
    section, rank = lax.axis_index("section"), lax.axis_index("dp")
    streams = []
    for i in range(6):
        streams.append(Stream(i, stream_refs[6 * i:6 * i + 6], sems, x_sems, z_sems))
    a_small, a_large, g_small, g_large, d_top, d_low = streams

    xs[0] = act_ref[...]
    grads[...] = cot_ref[...]
    gather_weights(w_ref, w_buf, *gather_refs)
    run_ahead(w_buf, xs, slopes, scales, units)
    u_own, dh_own = units.at[section], slants.at[section]

    def factor(ref, small, large):
        keep(small.part, 0, dot(ref[:, :HALF], ref[:, :HALF], (0, 0)))
        keep(large.part, 0, dot(ref[:, HALF:], ref[:, :HALF], (0, 0)))
        keep(large.part, WIDTH, dot(ref[:, HALF:], ref[:, HALF:], (0, 0)))

    def advance(group, t):
        for stream in group:
            stream.advance(t)

    in_pair, out_pair, d_pair = streams[:2], streams[2:4], streams[4:]
    factor(u_own, a_small, a_large)
    advance(in_pair, 0)

    def beside_back(step):
        for t, at in ((1, 2), (2, 5)):
            pl.when(step == at)(functools.partial(advance, in_pair, t))

    run_back(w_buf, xs, slopes, scales, grads, slants, beside_back)
    factor(dh_own, g_small, g_large)
    advance(out_pair, 0)
    keep(d_top.part, 0, dot(u_own[:, :HALF], dh_own[...], (0, 0)))
    keep(d_low.part, 0, dot(u_own[:, HALF:], dh_own[...], (0, 0)))
    for t in range(1, 7):
        advance(out_pair, t)
        if t + 2 <= 6:
            advance(in_pair, t + 2)
        if t + 2 == 6:
            load_factor(mats, 0, a_small.full, a_large.full)
        advance(d_pair, t - 1)
    load_factor(mats, 1, g_small.full, g_large.full)

    def beside_invert(step):
        if step == 2:
            advance(d_pair, 6)

    invert(mats, beside_invert)
    d_mat = jnp.concatenate([packed(d_top.full), packed(d_low.full)], axis=0)
    p_mat[...] = product_of_halves(mats[0], d_mat)
    p_mat[...] = product_of_halves(p_mat[...], mats[1])
    whole = p_mat[...]
    mean = jnp.sum(jnp.sum(whole * whole, axis=0, keepdims=True), axis=1, keepdims=True) * (1.0 / (WIDTH * WIDTH))
    mine = p_mat[pl.ds(pl.multiple_of(rank * 8, 8), 8), :]
    out_ref[...] = mine / jnp.sqrt(mean + 1e-06)
    for stream in streams:
        stream.close()


def local(first_acts, cotangent, weights):
    square = lambda n, kind: pltpu.VMEM((n, TOKENS, WIDTH), kind)
    flat = lambda kind: pltpu.VMEM((TOKENS, WIDTH), kind)
    copies = pltpu.SemaphoreType.DMA
    scratch = [
        pltpu.VMEM((2, 4, 2, 4, 128, HALF), jnp.bfloat16),
        square(LAYERS + 1, jnp.bfloat16),
        square(LAYERS, jnp.float32),
        pltpu.VMEM((LAYERS, TOKENS, 128), jnp.float32),
        flat(jnp.bfloat16), square(LAYERS, jnp.bfloat16), square(LAYERS, jnp.bfloat16),
        square(2, jnp.float32), flat(jnp.float32),
        pltpu.VMEM((8, HALF), jnp.float32),
        pltpu.VMEM((8, HALF), jnp.float32),
        copies((2,)), copies((16,)), copies((16,)),
        copies((4, 16)), copies((4, 16)), copies((4, 16)), copies((4, 16)),
        copies((2, 6, 2)), copies((2, 2, 6, 4)), copies((2, 2, 6, 8)),
    ]
    for rows in (512, 1024, 512, 1024, 1024, 1024):
        sizes = [rows, rows // 2, rows, rows // 2]
        scratch += [pltpu.VMEM((size, 128), jnp.float32) for size in sizes]
        scratch += [pltpu.VMEM((n - 1, rows // (2 * part), 128), jnp.float32) for n, part in ((4, 4), (8, 32))]
    return pl.pallas_call(
        kernel,
        out_shape=jax.ShapeDtypeStruct((8, WIDTH), jnp.float32),
        in_specs=[pl.BlockSpec(memory_space=pltpu.VMEM)] * 3,
        out_specs=pl.BlockSpec(memory_space=pltpu.VMEM),
        scratch_shapes=scratch,
        compiler_params=pltpu.CompilerParams(
            collective_id=0, has_side_effects=True, vmem_limit_bytes=VMEM_LIMIT
        ),
        name="chain_and_factors",
    )(first_acts.reshape(TOKENS, WIDTH), cotangent.reshape(TOKENS, WIDTH), weights)


def solution(mesh):
    placed = (P(None, "dp", None), P(None, "dp", None), P(("section", "dp"), None))
    return jax.shard_map(
        local, mesh=mesh, in_specs=placed, out_specs=P(("section", "dp"), None), check_vma=False
    )
```
